768 devices in a mesh: gx: 96 (over y, z), gy: 8 (over x, core).
Axes of the slice: x: 4, y: 8, z: 12, core: 2. Of those that a mesh axis runs over, the one named last changes fastest.
Arguments:
- members: bfloat16 [6144, 512, 128], P('gx', 'gy'), may hold values from -6 to 6
- courant: float32 [2, 6144, 512], P(None, 'gx', 'gy'), may hold values from -0.4 to 0.4
- obs_cells: int32 [96, 8, 128], P('gx', 'gy'), may hold values from 0 to 4095
- obs_count: int32 [96, 8], P('gx', 'gy'), may hold values from 64 to 128, as said below
- obs_value: float32 [96, 8, 128], P('gx', 'gy'), may hold values from -6 to 6
- obs_weight: float32 [96, 8, 128], P('gx', 'gy'), may hold values from 0.5 to 4
Outputs:
- analysis_mean: float32 [6144, 512], P('gx', 'gy')
- analysis_anomalies: bfloat16 [6144, 512, 128], P('gx', 'gy')
The draws below stay inside these ranges and needn't reach their ends.
Inputs may be any that keep to these rules, and one draw needn't show every extreme that they name: The first obs_count slots of each tile are live; some tile has all 128 live, some tile exactly 64.
All inputs are finite; a program needn't handle non-finite values.
Results may differ from the reference program's by a relative error of at most 0.001.
Values sent between devices are 32-bit elements; how exact they have to be, the bound alone decides.
A program may use at most 32 MiB of HBM per device.

```python
import math
import jax
import jax.numpy as jnp
from jax import lax

M = 128
CX = 64
CY = 64
OBS_DEV = 128
STEPS = 3
NX = 6144
NY = 512
TOTAL_OBS = 98304
N_GX = 96
N_GY = 8


def draw_obs_count(key, part):
    tile_total = N_GX * N_GY
    counts = jax.random.randint(jax.random.fold_in(key, 11), (tile_total,), OBS_DEV // 2, OBS_DEV + 1)
    chosen = jax.random.randint(jax.random.fold_in(key, 12), (), 0, tile_total)
    counts = counts.at[chosen].set(OBS_DEV)
    counts = counts.at[(chosen + 1) % tile_total].set(OBS_DEV // 2)
    return counts.reshape(N_GX, N_GY).astype(jnp.int32)


def place_ends(drawn, own_key, smallest, largest):
    longest = drawn.shape.index(max(drawn.shape))
    spots = []
    for shift in (0, 1):
        where = [jax.random.randint(jax.random.fold_in(own_key, axis), (), 0, length) for axis, length in enumerate(drawn.shape)]
        where[longest] = (where[longest] + shift) % drawn.shape[longest]
        spots.append(tuple(where))
    return drawn.at[spots[0]].set(smallest).at[spots[1]].set(largest)


def shard_levels(own_key, extent, shards, low, top_value):
    gain = 1.0
    for position, shards_of in shards:
        steps = jax.random.uniform(jax.random.fold_in(jax.random.fold_in(own_key, 6), position), (shards_of,), jnp.float32, low / len(shards), top_value / len(shards))
        gain = gain * jnp.repeat(jnp.exp(steps), extent[position] // shards_of).reshape((-1,) + (1,) * (len(extent) - 1 - position))
    return gain


def gaussian(rng, extent, scale, reach, shards=(), kind=jnp.bfloat16):
    values = jax.random.normal(rng, extent, jnp.float32) * scale
    if len(shards) > 0:
        values = shard_levels(rng, extent, shards, -0.22, 0.18) * values
    return jnp.clip(values, min=-reach, max=reach).astype(kind)


def setup_inputs(seed: int = 0) -> dict:
    streams_of = jax.random.split(jax.random.key(seed), 7)
    return {
        "members": gaussian(streams_of[0], (NX, NY, M), 1.0, 6.0, ((0, 96), (1, 8))),
        "courant": jnp.clip(jax.random.uniform(streams_of[1], (2, NX, NY), jnp.float32, -0.4, 0.4) * shard_levels(streams_of[1], (2, NX, NY), ((1, 96), (2, 8)), -0.4, 0.0), -0.4, 0.4),
        "obs_cells": place_ends(jax.random.randint(streams_of[2], (N_GX, N_GY, OBS_DEV), 0, CX * CY), jax.random.fold_in(streams_of[2], 1), 0, (CX * CY) - 1).astype(jnp.int32),
        "obs_count": draw_obs_count(jax.random.fold_in(streams_of[6], 71), 0),
        "obs_value": gaussian(streams_of[4], (N_GX, N_GY, OBS_DEV), 1.0, 6.0, ((0, 96), (1, 8)), jnp.float32),
        "obs_weight": jnp.clip(jnp.exp(math.log(4.0) - 2.0794415 * jax.random.uniform(streams_of[5], (N_GX, N_GY, OBS_DEV), jnp.float32) ** shard_levels(streams_of[5], (N_GX, N_GY, OBS_DEV), ((0, 96), (1, 8)), -0.2, 0.2)), 0.5, 4.0),
    }


diffusion = 0.2

def advance(padded_field, courant_part):
    centre = padded_field[1:-1, 1:-1]
    east_side = padded_field[2:, 1:-1]
    west_side = padded_field[:-2, 1:-1]
    north_side = padded_field[1:-1, 2:]
    south_side = padded_field[1:-1, :-2]
    return centre + diffusion * (east_side + west_side + north_side + south_side - 4.0 * centre) - 0.5 * courant_part[0][..., None] * (east_side - west_side) - 0.5 * courant_part[1][..., None] * (north_side - south_side)

def predicted_block(block_region, courant):
    for rotation_index in range(STEPS):
        block_region = advance(jnp.pad(block_region, ((1, 1), (1, 1), (0, 0))), courant)
    return block_region

def reference(members, courant, obs_cells, obs_count, obs_value, obs_weight):
    block_span_width = M // 8
    block_portions = [predicted_block(members[:, :, member_position * block_span_width:(member_position + 1) * block_span_width].astype(jnp.float32), courant) for member_position in range(8)]
    ensemble = jnp.concatenate(block_portions, axis=2)
    ensemble_average = lax.optimization_barrier(jnp.sum(ensemble, axis=2)) / M
    anomaly = ensemble - ensemble_average[..., None]
    tile_x = jnp.arange(N_GX, dtype=jnp.int32)[:, None, None]
    tile_y = jnp.arange(N_GY, dtype=jnp.int32)[None, :, None]
    grid_rows = tile_x * CX + obs_cells // CY
    grid_cols = tile_y * CY + obs_cells % CY
    observed = anomaly[grid_rows, grid_cols]
    obs_mean = ensemble_average[grid_rows, grid_cols]
    active_buffer_slot = jnp.arange(OBS_DEV, dtype=jnp.int32)[None, None, :] < obs_count[..., None]
    scale_factor = obs_weight / math.sqrt(TOTAL_OBS)
    scaled = jnp.where(active_buffer_slot[..., None], scale_factor[..., None] * observed, 0.0).reshape(-1, M)
    innovation = jnp.where(active_buffer_slot, obs_weight * (obs_value - obs_mean), 0.0).reshape(-1)
    gram_total = jnp.dot(scaled.T, scaled, precision=lax.Precision.HIGHEST) + jnp.eye(M, dtype=jnp.float32)
    cross_term = jnp.dot(scaled.T, innovation, precision=lax.Precision.HIGHEST)
    lower_factor = jnp.linalg.cholesky(gram_total)
    weights = jax.scipy.linalg.cho_solve((lower_factor, True), cross_term)
    flat_anomaly = anomaly.reshape(-1, M)
    analysis_mean = ensemble_average + jnp.dot(flat_anomaly, weights, precision=lax.Precision.HIGHEST).reshape(NX, NY)

    def solve_tile(tile_rows):
        return jax.scipy.linalg.solve_triangular(lower_factor, tile_rows.T, lower=True).T.astype(jnp.bfloat16)
    solved = lax.map(solve_tile, flat_anomaly.reshape(N_GX, CX * NY, M))
    return (analysis_mean, solved.reshape(NX, NY, M))
```

```python
import functools
import math

import jax
import jax.numpy as jnp
from jax import lax
from jax.experimental import pallas as pl
from jax.experimental.pallas import tpu as pltpu
from jax.sharding import PartitionSpec as P

M = 128
GROUPS = M // 8


def split(x):
    hi = x.astype(jnp.bfloat16)
    return hi, (x - hi.astype(jnp.float32)).astype(jnp.bfloat16)


def row_of(x, k):
    return jnp.broadcast_to(x[k : k + 1, :], x.shape)


def column_of(x, k):
    return jnp.broadcast_to(x[:, k : k + 1], (x.shape[0], 128))


def inverse_factor(gram_rows):
    sub = lax.broadcasted_iota(jnp.int32, (8, 128), 0)
    lane = lax.broadcasted_iota(jnp.int32, (8, 128), 1)
    a = [g + (lane == sub + 8 * i).astype(jnp.float32) for i, g in enumerate(gram_rows)]
    x = [(lane == sub + 8 * i).astype(jnp.float32) for i in range(GROUPS)]
    for p in range(GROUPS):
        c = [column_of(a[p], 8 * p + j) for j in range(8)]
        recip, upper, row_a, row_x = [], [], [], []
        pivots = jnp.ones((8, 128), jnp.float32)
        for k in range(8):
            pivot = row_of(c[k], k)
            r = 1.0 / pivot
            pivots = jnp.where(sub == k, pivot, pivots)
            recip.append(r)
            m = jnp.where(sub > k, c[k] * r, 0.0)
            upper.append([None] * 8)
            for j in range(k + 1, 8):
                upper[k][j] = row_of(c[j], k)
                c[j] = c[j] - m * upper[k][j]
            row_a.append(row_of(a[p], k))
            row_x.append(row_of(x[p], k))
            if k < 7:
                a[p] = a[p] - m * row_a[k]
                x[p] = x[p] - m * row_x[k]
        for i in range(p + 1, GROUPS):
            e = [column_of(a[i], 8 * p + j) for j in range(8)]
            for k in range(8):
                m = e[k] * recip[k]
                for j in range(k + 1, 8):
                    e[j] = e[j] - m * upper[k][j]
                a[i] = a[i] - m * row_a[k]
                x[i] = x[i] - m * row_x[k]
        x[p] = x[p] * lax.rsqrt(pivots)
    return x


def transform_kernel(rows, gram_ref, anom_hbm, mean_ref, out_mean, out_hbm, anom, out, mix, flat, sem_in, sem_out):
    chunks = 4
    cells = anom.shape[0] // chunks
    load = pltpu.make_async_copy(anom_hbm, anom, sem_in)
    load.start()
    groups = []
    for i in range(GROUPS):
        piece, start = divmod(8 * i, rows)
        groups.append(gram_ref[piece, start : start + 8, :])
    x = inverse_factor(groups)
    cross = jnp.broadcast_to(gram_ref[0, rows : rows + 1, :], (8, 128))
    total = jnp.zeros((8, 128), jnp.float32)
    for i in range(GROUPS):
        y = jnp.sum(x[i] * cross, axis=1, keepdims=True)
        total = total + x[i] * y
    weights = jnp.broadcast_to(jnp.sum(total, axis=0, keepdims=True), (16, 128))
    for i in range(0, GROUPS, 2):
        hi, lo = split(jnp.concatenate([x[i], x[i + 1]], axis=0))
        mix[8 * i : 8 * i + 16, 0:128] = hi
        mix[8 * i : 8 * i + 16, 128:256] = hi
        mix[128 + 8 * i : 128 + 8 * i + 16, 0:128] = lo
        mix[128 + 8 * i : 128 + 8 * i + 16, 128:256] = jnp.zeros((16, 128), jnp.bfloat16)
    w_hi, w_lo = split(weights)
    w_both = jnp.concatenate([w_hi, w_hi], axis=1)
    w_low = jnp.concatenate([w_lo, jnp.zeros_like(w_lo)], axis=1)
    w_rows = jnp.concatenate([w_both, w_low], axis=0)
    load.wait()
    nt = (((1,), (1,)), ((), ()))
    for q in range(chunks):
        part = pl.ds(q * cells, cells)
        block = anom[part, :]
        both = lax.dot_general(block, mix[...], nt, preferred_element_type=jnp.float32)
        out[part, :] = (both[:, 0:128] + both[:, 128:256]).astype(jnp.bfloat16)
        pltpu.make_async_copy(out.at[part], out_hbm.at[part], sem_out.at[q]).start()
    for q in range(chunks):
        part = pl.ds(q * cells, cells)
        shift = lax.dot_general(w_rows, anom[part, :], nt, preferred_element_type=jnp.float32)
        line = shift[0:1, :] + shift[16:17, :]
        for i in range(cells // 128):
            n = q * (cells // 128) + i
            flat[n : n + 1, :] = line[:, 128 * i : 128 * i + 128]
    lines = flat[...]
    ny = out_mean.shape[1]
    half = flat.shape[0]
    even = lines[:, 0:ny]
    odd = pltpu.roll(lines, 128 - ny, axis=1)[:, 0:ny]
    out_mean[pl.ds(0, half, stride=2), :] = mean_ref[pl.ds(0, half, stride=2), :] + even
    out_mean[pl.ds(1, half, stride=2), :] = mean_ref[pl.ds(1, half, stride=2), :] + odd
    for q in range(chunks):
        part = pl.ds(q * cells, cells)
        pltpu.make_async_copy(out.at[part], out_hbm.at[part], sem_out.at[q]).wait()


def transform(gram, anom, mean):
    pieces, piece_rows, _ = gram.shape
    cells = anom.shape[0]
    return pl.pallas_call(
        functools.partial(transform_kernel, piece_rows - 1),
        out_shape=(
            jax.ShapeDtypeStruct(mean.shape, jnp.float32),
            jax.ShapeDtypeStruct((cells, M), jnp.bfloat16),
        ),
        in_specs=[
            pl.BlockSpec(memory_space=pltpu.VMEM),
            pl.BlockSpec(memory_space=pl.ANY),
            pl.BlockSpec(memory_space=pltpu.VMEM),
        ],
        out_specs=(pl.BlockSpec(memory_space=pltpu.VMEM), pl.BlockSpec(memory_space=pl.ANY)),
        scratch_shapes=[
            pltpu.VMEM((cells, 2 * M), jnp.bfloat16),
            pltpu.VMEM((cells, M), jnp.bfloat16),
            pltpu.VMEM((2 * M, 2 * M), jnp.bfloat16),
            pltpu.VMEM((cells // 128, 128), jnp.float32),
            pltpu.SemaphoreType.DMA,
            pltpu.SemaphoreType.DMA((4,)),
        ],
        compiler_params=pltpu.CompilerParams(vmem_limit_bytes=24 * 2**20),
    )(gram, anom, mean)


STEPS = 3
SIDE = 64
PITCH = 80
EDGE = 8
DIFFUSION = 0.2
HIGHEST = lax.Precision.HIGHEST
MESH = pl.DeviceIdType.MESH


def forecast_kernel(
    nz, total_slots,
    members_hbm, courant_ref, cells_ref, count_ref, value_ref, weight_ref,
    gram_out, anom_hbm, mean_out,
    members, state0, state1, state2, state3, along, across, column_out, column_in,
    observed, anom, parts, from_gy, held_y, from_y, held_z, from_z, held_gy, whole,
    sem_members, sem_anom, halo_send, halo_recv, gy_send, gy_recv, y_send, y_recv, z_send, z_recv, back_send, back_recv,
):
    states = [state0, state1, state2, state3]
    gx, gy = lax.axis_index("gx"), lax.axis_index("gy")
    n_gx, n_gy = lax.axis_size("gx"), lax.axis_size("gy")
    ny = n_gx // nz
    y, z = gx // nz, lax.rem(gx, nz)
    has_west, has_east, has_south, has_north = gx > 0, gx < n_gx - 1, gy > 0, gy < n_gy - 1

    load = pltpu.make_async_copy(members_hbm, members, sem_members)
    load.start()

    barrier = pltpu.get_barrier_semaphore()

    def greet(count, peer_of):
        def body(i, carry):
            pl.semaphore_signal(barrier, inc=1, device_id=peer_of(i), device_id_type=MESH)
            return carry
        lax.fori_loop(1, count, body, 0)

    def gy_peer(i):
        return lax.rem(gy + i, n_gy)

    def y_peer(i):
        return lax.rem(y + i, ny)

    def z_peer(i):
        return lax.rem(z + i, nz)

    greet(n_gy, lambda i: (gx, gy_peer(i)))
    greet(ny, lambda i: (y_peer(i) * nz + z, gy))
    greet(nz, lambda i: (y * nz + z_peer(i), gy))
    far_west = jnp.logical_and(has_west, z == 0)
    far_east = jnp.logical_and(has_east, z == nz - 1)

    @pl.when(far_west)
    def _():
        pl.semaphore_signal(barrier, inc=1, device_id=(gx - 1, gy), device_id_type=MESH)

    @pl.when(far_east)
    def _():
        pl.semaphore_signal(barrier, inc=1, device_id=(gx + 1, gy), device_id_type=MESH)

    zeros = jnp.zeros((SIDE, 128), jnp.float32)
    low_row, high_row = pl.ds(EDGE, SIDE), pl.ds((SIDE + 1) * PITCH + EDGE, SIDE)
    first_row, last_row = pl.ds(PITCH + EDGE, SIDE), pl.ds(SIDE * PITCH + EDGE, SIDE)

    def column(cell, shift=0):
        return pl.ds((1 + shift) * PITCH + EDGE + cell, SIDE, stride=PITCH)

    for step in range(STEPS):
        @pl.when(jnp.logical_not(has_west))
        def _():
            states[step][low_row, :] = zeros

        @pl.when(jnp.logical_not(has_east))
        def _():
            states[step][high_row, :] = zeros

        @pl.when(jnp.logical_not(has_south))
        def _():
            column_in[step, 0] = zeros

        @pl.when(jnp.logical_not(has_north))
        def _():
            column_in[step, 1] = zeros

    load.wait()

    def fill(i, carry):
        state0[pl.ds(pl.multiple_of((i + 1) * PITCH + EDGE, 8), SIDE), :] = members[
            pl.ds(pl.multiple_of(i * SIDE, SIDE), SIDE), :
        ].astype(jnp.float32)
        return carry

    lax.fori_loop(0, SIDE, fill, 0)
    column_out[0, 0] = state0[column(0), :]
    column_out[0, 1] = state0[column(SIDE - 1), :]

    pl.semaphore_wait(
        barrier,
        (n_gy - 1) + (ny - 1) + (nz - 1) + far_west.astype(jnp.int32) + far_east.astype(jnp.int32),
    )

    def halo_copies(step):
        state = states[step]
        west = pltpu.make_async_remote_copy(
            src_ref=state.at[first_row], dst_ref=state.at[high_row],
            send_sem=halo_send.at[step, 0], recv_sem=halo_recv.at[step, 1],
            device_id=(gx - 1, gy), device_id_type=MESH,
        )
        east = pltpu.make_async_remote_copy(
            src_ref=state.at[last_row], dst_ref=state.at[low_row],
            send_sem=halo_send.at[step, 1], recv_sem=halo_recv.at[step, 0],
            device_id=(gx + 1, gy), device_id_type=MESH,
        )
        south = pltpu.make_async_remote_copy(
            src_ref=column_out.at[step, 0], dst_ref=column_in.at[step, 1],
            send_sem=halo_send.at[step, 2], recv_sem=halo_recv.at[step, 3],
            device_id=(gx, gy - 1), device_id_type=MESH,
        )
        north = pltpu.make_async_remote_copy(
            src_ref=column_out.at[step, 1], dst_ref=column_in.at[step, 0],
            send_sem=halo_send.at[step, 3], recv_sem=halo_recv.at[step, 2],
            device_id=(gx, gy + 1), device_id_type=MESH,
        )
        return west, east, south, north

    def start_halo(step):
        copies = halo_copies(step)
        for there, copy in zip((has_west, has_east, has_south, has_north), copies):
            @pl.when(there)
            def _():
                copy.start()

    def finish_halo(step):
        west, east, south, north = halo_copies(step)
        for there, out, back in (
            (has_west, west, east), (has_east, east, west), (has_south, south, north), (has_north, north, south)
        ):
            @pl.when(there)
            def _():
                back.wait_recv()
                out.wait_send()

    start_halo(0)

    eye_x = lax.broadcasted_iota(jnp.int32, (SIDE, SIDE), 0)
    eye_y = lax.broadcasted_iota(jnp.int32, (SIDE, SIDE), 1)
    eye = eye_x == eye_y

    def spread(i, carry):
        rows = pl.ds(pl.multiple_of(i * SIDE, SIDE), SIDE)
        for which, target in ((0, along), (1, across)):
            line = courant_ref[which, pl.ds(i, 1), :] * (0.5 / DIFFUSION)
            tall = jnp.sum(jnp.where(eye, line, 0.0), axis=1, keepdims=True)
            target[rows, :] = jnp.broadcast_to(tall, (SIDE, 128))
        return carry

    lax.fori_loop(0, SIDE, spread, 0)

    def update(state, at, flow_at):
        centre, east, west, north, south = (state[s, :] for s in at)
        return (
            ((east + west) + (north + south) + centre)
            - along[flow_at, :] * (east - west)
            - across[flow_at, :] * (north - south)
        )

    last_scale = DIFFUSION**STEPS

    def advance_row(step, i):
        base = (i + 1) * PITCH + EDGE
        if not isinstance(base, int):
            base = pl.multiple_of(base, 8)
        shifts = (0, PITCH, -PITCH, 1, -1)
        at = [pl.ds(base + s, SIDE) for s in shifts]
        flow = i * SIDE
        if not isinstance(flow, int):
            flow = pl.multiple_of(flow, SIDE)
        out = update(states[step], at, pl.ds(flow, SIDE))
        if step == STEPS - 1:
            out = out * last_scale
        states[step + 1][at[0], :] = out

    def advance_column(step, cell, side):
        at = [column(cell), column(cell, 1), column(cell, -1), column(cell + 1), column(cell - 1)]
        column_out[step + 1, side] = update(states[step], at, pl.ds(cell, SIDE, stride=SIDE))

    for step in range(STEPS):
        finish_halo(step)
        states[step][column(-1), :] = column_in[step, 0]
        states[step][column(SIDE), :] = column_in[step, 1]
        advance_row(step, 0)
        advance_row(step, SIDE - 1)
        if step + 1 < STEPS:
            advance_column(step, 0, 0)
            advance_column(step, SIDE - 1, 1)
            start_halo(step + 1)

        def interior(i, carry, step=step):
            advance_row(step, i)
            return carry

        lax.fori_loop(1, SIDE - 1, interior, 0)

    slots = observed.shape[0]

    def pick(s, carry):
        cell = cells_ref[0, s]
        row = (cell // SIDE + 1) * PITCH + EDGE + lax.rem(cell, SIDE)
        observed[pl.ds(s, 1), :] = state3[pl.ds(row, 1), :]
        return carry

    lax.fori_loop(0, slots, pick, 0, unroll=8)

    seen = observed[...].T
    members_total = seen.shape[0]
    seen_mean = jnp.sum(seen, axis=0, keepdims=True) / members_total
    live = lax.broadcasted_iota(jnp.int32, (1, slots), 1) < count_ref[0, 0]
    weight = weight_ref[...]
    scaled = (seen - seen_mean) * jnp.where(live, weight / math.sqrt(total_slots), 0.0)
    innovation = jnp.where(live, weight * (value_ref[...] - seen_mean), 0.0)
    left = jnp.concatenate([scaled, jnp.broadcast_to(innovation, (8, slots))], axis=0)
    nt = (((1,), (1,)), ((), ()))
    gram = lax.dot_general(left, scaled, nt, precision=HIGHEST, preferred_element_type=jnp.float32)
    rows = members_total // n_gy
    for j in range(n_gy):
        parts[j, 0:rows, :] = gram[j * rows : (j + 1) * rows, :]
        parts[j, rows : rows + 1, :] = gram[members_total : members_total + 1, :]

    def exchange(count, me, peer, device, source, target, send, recv):
        def copy(i, slot):
            return pltpu.make_async_remote_copy(
                src_ref=source(peer(i)), dst_ref=target.at[slot],
                send_sem=send.at[peer(i)], recv_sem=recv.at[slot],
                device_id=device(peer(i)), device_id_type=MESH,
            )

        def begin():
            def body(i, carry):
                copy(i, me).start()
                return carry
            lax.fori_loop(1, count, body, 0)

        def end():
            def body(i, carry):
                copy(i, peer(i)).wait_recv()
                copy(i, me).wait_send()
                return carry
            lax.fori_loop(1, count, body, 0)

        return begin, end

    def total(ref, count):
        out = ref[0]
        for j in range(1, count):
            out = out + ref[j]
        return out

    gy_begin, gy_end = exchange(
        n_gy, gy, gy_peer, lambda p: (gx, p), lambda p: parts.at[p], from_gy, gy_send, gy_recv
    )
    y_begin, y_end = exchange(
        ny, y, y_peer, lambda p: (p * nz + z, gy), lambda p: held_y, from_y, y_send, y_recv
    )
    z_begin, z_end = exchange(
        nz, z, z_peer, lambda p: (y * nz + p, gy), lambda p: held_z, from_z, z_send, z_recv
    )
    back_begin, back_end = exchange(
        n_gy, gy, gy_peer, lambda p: (gx, p), lambda p: held_gy, whole, back_send, back_recv
    )

    def anomalies(i, carry):
        block = state3[pl.ds(pl.multiple_of((i + 1) * PITCH + EDGE, 8), SIDE), :]
        average = jnp.sum(block, axis=1, keepdims=True) / members_total
        hi, lo = split(block - average)
        at = pl.ds(pl.multiple_of(i * SIDE, SIDE), SIDE)
        anom[at, 0:128] = hi
        anom[at, 128:256] = lo
        mean_out[pl.ds(i, 1), :] = jnp.sum(jnp.where(eye, average, 0.0), axis=0, keepdims=True)
        return carry

    gy_begin()
    from_gy[gy] = parts[gy]
    lax.fori_loop(0, SIDE // 2, anomalies, 0)
    gy_end()
    held_y[...] = total(from_gy, n_gy)
    y_begin()
    from_y[y] = held_y[...]
    lax.fori_loop(SIDE // 2, SIDE, anomalies, 0)
    store = pltpu.make_async_copy(anom, anom_hbm, sem_anom)
    store.start()
    y_end()
    held_z[...] = total(from_y, ny)
    z_begin()
    from_z[z] = held_z[...]
    z_end()
    held_gy[...] = total(from_z, nz)
    back_begin()
    whole[gy] = held_gy[...]
    back_end()
    gram_out[...] = whole[...]
    store.wait()


def forecast(nz, n_gx, n_gy, members, courant, cells, count, value, weight):
    ny = n_gx // nz
    piece = (128 // n_gy + 1, 128)
    f32 = jnp.float32
    state = pltpu.VMEM(((SIDE + 2) * PITCH, 128), f32)
    dma = pltpu.SemaphoreType.DMA
    vmem, smem, hbm = (pl.BlockSpec(memory_space=s) for s in (pltpu.VMEM, pltpu.SMEM, pl.ANY))
    return pl.pallas_call(
        functools.partial(forecast_kernel, nz, 128 * n_gx * n_gy),
        out_shape=(
            jax.ShapeDtypeStruct((n_gy,) + piece, f32),
            jax.ShapeDtypeStruct((SIDE * SIDE, 256), jnp.bfloat16),
            jax.ShapeDtypeStruct((SIDE, SIDE), f32),
        ),
        in_specs=[hbm, vmem, smem, smem, vmem, vmem],
        out_specs=(vmem, hbm, vmem),
        scratch_shapes=[
            pltpu.VMEM((SIDE * SIDE, 128), jnp.bfloat16),
            state, state, state, state,
            pltpu.VMEM((SIDE * SIDE, 128), f32),
            pltpu.VMEM((SIDE * SIDE, 128), f32),
            pltpu.VMEM((STEPS, 2, SIDE, 128), f32),
            pltpu.VMEM((STEPS, 2, SIDE, 128), f32),
            pltpu.VMEM((128, 128), f32),
            pltpu.VMEM((SIDE * SIDE, 256), jnp.bfloat16),
            pltpu.VMEM((n_gy,) + piece, f32),
            pltpu.VMEM((n_gy,) + piece, f32),
            pltpu.VMEM(piece, f32),
            pltpu.VMEM((ny,) + piece, f32),
            pltpu.VMEM(piece, f32),
            pltpu.VMEM((nz,) + piece, f32),
            pltpu.VMEM(piece, f32),
            pltpu.VMEM((n_gy,) + piece, f32),
            dma, dma,
            dma((STEPS, 4)), dma((STEPS, 4)),
            dma((n_gy,)), dma((n_gy,)),
            dma((ny,)), dma((ny,)),
            dma((nz,)), dma((nz,)),
            dma((n_gy,)), dma((n_gy,)),
        ],
        compiler_params=pltpu.CompilerParams(
            collective_id=0, has_side_effects=True, vmem_limit_bytes=40 * 2**20
        ),
    )(members, courant, cells, count, value, weight)


def shards(nz, n_gx, n_gy, members, courant, obs_cells, obs_count, obs_value, obs_weight):
    tile_rows, tile_cols, member_total = members.shape
    flat = members.reshape(tile_rows * tile_cols, member_total)
    gram, anom, mean = forecast(
        nz, n_gx, n_gy, flat, courant,
        obs_cells.reshape(1, -1), obs_count, obs_value.reshape(1, -1), obs_weight.reshape(1, -1),
    )
    out_mean, out_anom = transform(gram, anom, mean)
    return out_mean, out_anom.reshape(members.shape)


Z_CHIPS = 12


def solution(mesh):
    n_gx, n_gy = mesh.shape["gx"], mesh.shape["gy"]
    in_specs = (
        P("gx", "gy", None),
        P(None, "gx", "gy"),
        P("gx", "gy", None),
        P("gx", "gy"),
        P("gx", "gy", None),
        P("gx", "gy", None),
    )
    out_specs = (P("gx", "gy"), P("gx", "gy", None))
    body = functools.partial(shards, Z_CHIPS, n_gx, n_gy)
    return jax.shard_map(body, mesh=mesh, in_specs=in_specs, out_specs=out_specs, check_vma=False)
```

```python
import functools
import math

import jax
import jax.numpy as jnp
from jax import lax
from jax.experimental import pallas as pl
from jax.experimental.pallas import tpu as pltpu
from jax.sharding import PartitionSpec as P

M = 128
GROUPS = M // 8


def split(x):
    hi = x.astype(jnp.bfloat16)
    return hi, (x - hi.astype(jnp.float32)).astype(jnp.bfloat16)


def row_of(x, k):
    return jnp.broadcast_to(x[k : k + 1, :], x.shape)


def column_of(x, k):
    return jnp.broadcast_to(x[:, k : k + 1], (x.shape[0], 128))


def inverse_factor(gram_rows):
    sub = lax.broadcasted_iota(jnp.int32, (8, 128), 0)
    lane = lax.broadcasted_iota(jnp.int32, (8, 128), 1)
    a = [g + (lane == sub + 8 * i).astype(jnp.float32) for i, g in enumerate(gram_rows)]
    x = [(lane == sub + 8 * i).astype(jnp.float32) for i in range(GROUPS)]
    c = [column_of(a[0], j) for j in range(8)]
    for p in range(GROUPS):
        more = p + 1 < GROUPS
        if more:
            e = [column_of(a[p + 1], 8 * p + j) for j in range(8)]
            d = [column_of(a[p + 1], 8 * p + 8 + j) for j in range(8)]
        recip, upper, row_a, row_x = [], [], [], []
        pivots = jnp.ones((8, 128), jnp.float32)
        for k in range(8):
            pivot = row_of(c[k], k)
            r = 1.0 / pivot
            pivots = jnp.where(sub == k, pivot, pivots)
            recip.append(r)
            m = jnp.where(sub > k, c[k] * r, 0.0)
            upper.append([None] * 8)
            for j in range(k + 1, 8):
                upper[k][j] = row_of(c[j], k)
                c[j] = c[j] - m * upper[k][j]
            if more:
                n = e[k] * r
                for j in range(k + 1, 8):
                    e[j] = e[j] - n * upper[k][j]
                for j in range(8):
                    d[j] = d[j] - n * row_of(e[k], j)
            row_a.append(row_of(a[p], k))
            row_x.append(row_of(x[p], k))
            if k < 7:
                a[p] = a[p] - m * row_a[k]
                x[p] = x[p] - m * row_x[k]
            if more:
                a[p + 1] = a[p + 1] - n * row_a[k]
                x[p + 1] = x[p + 1] - n * row_x[k]
        for i in range(p + 2, GROUPS):
            f = [column_of(a[i], 8 * p + j) for j in range(8)]
            for k in range(8):
                m = f[k] * recip[k]
                for j in range(k + 1, 8):
                    f[j] = f[j] - m * upper[k][j]
                a[i] = a[i] - m * row_a[k]
                x[i] = x[i] - m * row_x[k]
        x[p] = x[p] * lax.rsqrt(pivots)
        if more:
            c = d
    return x


def transform_kernel(rows, gram_ref, anom_hbm, mean_ref, out_mean, out_hbm, anom, out, mix, flat, sem_in, sem_out):
    chunks = 4
    cells = anom.shape[0] // chunks
    load = pltpu.make_async_copy(anom_hbm, anom, sem_in)
    load.start()
    groups = []
    for i in range(GROUPS):
        piece, start = divmod(8 * i, rows)
        groups.append(gram_ref[piece, start : start + 8, :])
    x = inverse_factor(groups)
    cross = jnp.broadcast_to(gram_ref[0, rows : rows + 1, :], (8, 128))
    total = jnp.zeros((8, 128), jnp.float32)
    for i in range(GROUPS):
        y = jnp.sum(x[i] * cross, axis=1, keepdims=True)
        total = total + x[i] * y
    weights = jnp.broadcast_to(jnp.sum(total, axis=0, keepdims=True), (16, 128))
    for i in range(0, GROUPS, 2):
        hi, lo = split(jnp.concatenate([x[i], x[i + 1]], axis=0))
        mix[8 * i : 8 * i + 16, 0:128] = hi
        mix[8 * i : 8 * i + 16, 128:256] = hi
        mix[128 + 8 * i : 128 + 8 * i + 16, 0:128] = lo
        mix[128 + 8 * i : 128 + 8 * i + 16, 128:256] = jnp.zeros((16, 128), jnp.bfloat16)
    w_hi, w_lo = split(weights)
    w_both = jnp.concatenate([w_hi, w_hi], axis=1)
    w_low = jnp.concatenate([w_lo, jnp.zeros_like(w_lo)], axis=1)
    w_rows = jnp.concatenate([w_both, w_low], axis=0)
    load.wait()
    nt = (((1,), (1,)), ((), ()))
    for q in range(chunks):
        part = pl.ds(q * cells, cells)
        block = anom[part, :]
        both = lax.dot_general(block, mix[...], nt, preferred_element_type=jnp.float32)
        out[part, :] = (both[:, 0:128] + both[:, 128:256]).astype(jnp.bfloat16)
        pltpu.make_async_copy(out.at[part], out_hbm.at[part], sem_out.at[q]).start()
    for q in range(chunks):
        part = pl.ds(q * cells, cells)
        shift = lax.dot_general(w_rows, anom[part, :], nt, preferred_element_type=jnp.float32)
        line = shift[0:1, :] + shift[16:17, :]
        for i in range(cells // 128):
            n = q * (cells // 128) + i
            flat[n : n + 1, :] = line[:, 128 * i : 128 * i + 128]
    lines = flat[...]
    ny = out_mean.shape[1]
    half = flat.shape[0]
    even = lines[:, 0:ny]
    odd = pltpu.roll(lines, 128 - ny, axis=1)[:, 0:ny]
    out_mean[pl.ds(0, half, stride=2), :] = mean_ref[pl.ds(0, half, stride=2), :] + even
    out_mean[pl.ds(1, half, stride=2), :] = mean_ref[pl.ds(1, half, stride=2), :] + odd
    for q in range(chunks):
        part = pl.ds(q * cells, cells)
        pltpu.make_async_copy(out.at[part], out_hbm.at[part], sem_out.at[q]).wait()


def transform(gram, anom, mean):
    pieces, piece_rows, _ = gram.shape
    cells = anom.shape[0]
    return pl.pallas_call(
        functools.partial(transform_kernel, piece_rows - 1),
        out_shape=(
            jax.ShapeDtypeStruct(mean.shape, jnp.float32),
            jax.ShapeDtypeStruct((cells, M), jnp.bfloat16),
        ),
        in_specs=[
            pl.BlockSpec(memory_space=pltpu.VMEM),
            pl.BlockSpec(memory_space=pl.ANY),
            pl.BlockSpec(memory_space=pltpu.VMEM),
        ],
        out_specs=(pl.BlockSpec(memory_space=pltpu.VMEM), pl.BlockSpec(memory_space=pl.ANY)),
        scratch_shapes=[
            pltpu.VMEM((cells, 2 * M), jnp.bfloat16),
            pltpu.VMEM((cells, M), jnp.bfloat16),
            pltpu.VMEM((2 * M, 2 * M), jnp.bfloat16),
            pltpu.VMEM((cells // 128, 128), jnp.float32),
            pltpu.SemaphoreType.DMA,
            pltpu.SemaphoreType.DMA((4,)),
        ],
        compiler_params=pltpu.CompilerParams(vmem_limit_bytes=24 * 2**20),
    )(gram, anom, mean)


STEPS = 3
SIDE = 64
PITCH = 80
EDGE = 8
DIFFUSION = 0.2
HIGHEST = lax.Precision.HIGHEST
MESH = pl.DeviceIdType.MESH


def forecast_kernel(
    nz, total_slots,
    members_hbm, courant_hbm, cells_hbm, count_ref, value_hbm, weight_hbm,
    gram_out, anom_hbm, mean_out,
    members, courant_ref, cells_ref, value_ref, weight_ref, state0, state1, state2, state3, along, across, column_out, column_in,
    observed, anom, parts, from_gy, held_y, from_y, held_z, from_z, held_gy, whole,
    sem_members, sem_small, sem_anom, halo_send, halo_recv, gy_send, gy_recv, y_send, y_recv, z_send, z_recv, back_send, back_recv,
):
    states = [state0, state1, state2, state3]
    gx, gy = lax.axis_index("gx"), lax.axis_index("gy")
    n_gx, n_gy = lax.axis_size("gx"), lax.axis_size("gy")
    ny = n_gx // nz
    y, z = gx // nz, lax.rem(gx, nz)
    has_west, has_east, has_south, has_north = gx > 0, gx < n_gx - 1, gy > 0, gy < n_gy - 1

    load = pltpu.make_async_copy(members_hbm, members, sem_members)
    load.start()
    smalls = [
        pltpu.make_async_copy(source, target, sem_small.at[i])
        for i, (source, target) in enumerate(
            (
                (courant_hbm, courant_ref),
                (cells_hbm, cells_ref),
                (value_hbm, value_ref),
                (weight_hbm, weight_ref),
            )
        )
    ]
    for small in smalls:
        small.start()

    barrier = pltpu.get_barrier_semaphore()

    def greet(count, peer_of):
        def body(i, carry):
            pl.semaphore_signal(barrier, inc=1, device_id=peer_of(i), device_id_type=MESH)
            return carry
        lax.fori_loop(1, count, body, 0)

    def gy_peer(i):
        return lax.rem(gy + i, n_gy)

    def y_peer(i):
        return lax.rem(y + i, ny)

    def z_peer(i):
        return lax.rem(z + i, nz)

    greet(n_gy, lambda i: (gx, gy_peer(i)))
    greet(ny, lambda i: (y_peer(i) * nz + z, gy))
    greet(nz, lambda i: (y * nz + z_peer(i), gy))
    far_west = jnp.logical_and(has_west, z == 0)
    far_east = jnp.logical_and(has_east, z == nz - 1)

    @pl.when(far_west)
    def _():
        pl.semaphore_signal(barrier, inc=1, device_id=(gx - 1, gy), device_id_type=MESH)

    @pl.when(far_east)
    def _():
        pl.semaphore_signal(barrier, inc=1, device_id=(gx + 1, gy), device_id_type=MESH)

    zeros = jnp.zeros((SIDE, 128), jnp.float32)
    low_row, high_row = pl.ds(EDGE, SIDE), pl.ds((SIDE + 1) * PITCH + EDGE, SIDE)
    first_row, last_row = pl.ds(PITCH + EDGE, SIDE), pl.ds(SIDE * PITCH + EDGE, SIDE)

    def column(cell, shift=0):
        return pl.ds((1 + shift) * PITCH + EDGE + cell, SIDE, stride=PITCH)

    for step in range(STEPS):
        @pl.when(jnp.logical_not(has_west))
        def _():
            states[step][low_row, :] = zeros

        @pl.when(jnp.logical_not(has_east))
        def _():
            states[step][high_row, :] = zeros

        @pl.when(jnp.logical_not(has_south))
        def _():
            column_in[step, 0] = zeros

        @pl.when(jnp.logical_not(has_north))
        def _():
            column_in[step, 1] = zeros

    load.wait()

    def fill(i, carry):
        state0[pl.ds(pl.multiple_of((i + 1) * PITCH + EDGE, 8), SIDE), :] = members[
            pl.ds(pl.multiple_of(i * SIDE, SIDE), SIDE), :
        ].astype(jnp.float32)
        return carry

    lax.fori_loop(0, SIDE, fill, 0, unroll=4)
    column_out[0, 0] = state0[column(0), :]
    column_out[0, 1] = state0[column(SIDE - 1), :]

    pl.semaphore_wait(
        barrier,
        (n_gy - 1) + (ny - 1) + (nz - 1) + far_west.astype(jnp.int32) + far_east.astype(jnp.int32),
    )

    def halo_copies(step):
        state = states[step]
        west = pltpu.make_async_remote_copy(
            src_ref=state.at[first_row], dst_ref=state.at[high_row],
            send_sem=halo_send.at[step, 0], recv_sem=halo_recv.at[step, 1],
            device_id=(gx - 1, gy), device_id_type=MESH,
        )
        east = pltpu.make_async_remote_copy(
            src_ref=state.at[last_row], dst_ref=state.at[low_row],
            send_sem=halo_send.at[step, 1], recv_sem=halo_recv.at[step, 0],
            device_id=(gx + 1, gy), device_id_type=MESH,
        )
        south = pltpu.make_async_remote_copy(
            src_ref=column_out.at[step, 0], dst_ref=column_in.at[step, 1],
            send_sem=halo_send.at[step, 2], recv_sem=halo_recv.at[step, 3],
            device_id=(gx, gy - 1), device_id_type=MESH,
        )
        north = pltpu.make_async_remote_copy(
            src_ref=column_out.at[step, 1], dst_ref=column_in.at[step, 0],
            send_sem=halo_send.at[step, 3], recv_sem=halo_recv.at[step, 2],
            device_id=(gx, gy + 1), device_id_type=MESH,
        )
        return west, east, south, north

    def start_halo(step):
        copies = halo_copies(step)
        for there, copy in zip((has_west, has_east, has_south, has_north), copies):
            @pl.when(there)
            def _():
                copy.start()

    def finish_halo(step):
        west, east, south, north = halo_copies(step)
        for there, out, back in (
            (has_west, west, east), (has_east, east, west), (has_south, south, north), (has_north, north, south)
        ):
            @pl.when(there)
            def _():
                back.wait_recv()
                out.wait_send()

    start_halo(0)
    smalls[0].wait()

    eye_x = lax.broadcasted_iota(jnp.int32, (SIDE, SIDE), 0)
    eye_y = lax.broadcasted_iota(jnp.int32, (SIDE, SIDE), 1)
    eye = eye_x == eye_y

    def spread(i, carry):
        rows = pl.ds(pl.multiple_of(i * SIDE, SIDE), SIDE)
        for which, target in ((0, along), (1, across)):
            line = courant_ref[which, pl.ds(i, 1), :] * (0.5 / DIFFUSION)
            tall = jnp.sum(jnp.where(eye, line, 0.0), axis=1, keepdims=True)
            target[rows, :] = jnp.broadcast_to(tall, (SIDE, 128))
        return carry

    lax.fori_loop(0, SIDE, spread, 0, unroll=8)

    def update(state, at, flow_at):
        centre, east, west, north, south = (state[s, :] for s in at)
        return (
            ((east + west) + (north + south) + centre)
            - along[flow_at, :] * (east - west)
            - across[flow_at, :] * (north - south)
        )

    last_scale = DIFFUSION**STEPS

    def advance_row(step, i):
        base = (i + 1) * PITCH + EDGE
        if not isinstance(base, int):
            base = pl.multiple_of(base, 8)
        shifts = (0, PITCH, -PITCH, 1, -1)
        at = [pl.ds(base + s, SIDE) for s in shifts]
        flow = i * SIDE
        if not isinstance(flow, int):
            flow = pl.multiple_of(flow, SIDE)
        out = update(states[step], at, pl.ds(flow, SIDE))
        if step == STEPS - 1:
            out = out * last_scale
        states[step + 1][at[0], :] = out

    def advance_column(step, cell, side):
        at = [column(cell), column(cell, 1), column(cell, -1), column(cell + 1), column(cell - 1)]
        column_out[step + 1, side] = update(states[step], at, pl.ds(cell, SIDE, stride=SIDE))

    for step in range(STEPS):
        finish_halo(step)
        states[step][column(-1), :] = column_in[step, 0]
        states[step][column(SIDE), :] = column_in[step, 1]
        advance_row(step, 0)
        advance_row(step, SIDE - 1)
        if step + 1 < STEPS:
            advance_column(step, 0, 0)
            advance_column(step, SIDE - 1, 1)
            start_halo(step + 1)

        def interior(i, carry, step=step):
            advance_row(step, i)
            return carry

        lax.fori_loop(1, SIDE - 1, interior, 0, unroll=2)

    slots = observed.shape[0]

    def pick(s, carry):
        cell = cells_ref[0, s]
        row = (cell // SIDE + 1) * PITCH + EDGE + lax.rem(cell, SIDE)
        observed[pl.ds(s, 1), :] = state3[pl.ds(row, 1), :]
        return carry

    for small in smalls[1:]:
        small.wait()
    lax.fori_loop(0, slots, pick, 0, unroll=8)

    seen = observed[...].T
    members_total = seen.shape[0]
    seen_mean = jnp.sum(seen, axis=0, keepdims=True) / members_total
    live = lax.broadcasted_iota(jnp.int32, (1, slots), 1) < count_ref[0, 0]
    weight = weight_ref[...]
    scaled = (seen - seen_mean) * jnp.where(live, weight / math.sqrt(total_slots), 0.0)
    innovation = jnp.where(live, weight * (value_ref[...] - seen_mean), 0.0)
    left = jnp.concatenate([scaled, jnp.broadcast_to(innovation, (8, slots))], axis=0)
    nt = (((1,), (1,)), ((), ()))
    gram = lax.dot_general(left, scaled, nt, precision=HIGHEST, preferred_element_type=jnp.float32)
    rows = members_total // n_gy
    for j in range(n_gy):
        parts[j, 0:rows, :] = gram[j * rows : (j + 1) * rows, :]
        parts[j, rows : rows + 1, :] = gram[members_total : members_total + 1, :]

    def exchange(count, me, peer, device, source, target, send, recv):
        def copy(i, slot):
            return pltpu.make_async_remote_copy(
                src_ref=source(peer(i)), dst_ref=target.at[slot],
                send_sem=send.at[peer(i)], recv_sem=recv.at[slot],
                device_id=device(peer(i)), device_id_type=MESH,
            )

        def begin():
            def body(i, carry):
                copy(i, me).start()
                return carry
            lax.fori_loop(1, count, body, 0)

        def end():
            def body(i, carry):
                copy(i, peer(i)).wait_recv()
                copy(i, me).wait_send()
                return carry
            lax.fori_loop(1, count, body, 0)

        return begin, end

    def total(ref, count):
        out = ref[0]
        for j in range(1, count):
            out = out + ref[j]
        return out

    gy_begin, gy_end = exchange(
        n_gy, gy, gy_peer, lambda p: (gx, p), lambda p: parts.at[p], from_gy, gy_send, gy_recv
    )
    y_begin, y_end = exchange(
        ny, y, y_peer, lambda p: (p * nz + z, gy), lambda p: held_y, from_y, y_send, y_recv
    )
    z_begin, z_end = exchange(
        nz, z, z_peer, lambda p: (y * nz + p, gy), lambda p: held_z, from_z, z_send, z_recv
    )
    back_begin, back_end = exchange(
        n_gy, gy, gy_peer, lambda p: (gx, p), lambda p: held_gy, whole, back_send, back_recv
    )

    def anomalies(i, carry):
        block = state3[pl.ds(pl.multiple_of((i + 1) * PITCH + EDGE, 8), SIDE), :]
        average = jnp.sum(block, axis=1, keepdims=True) / members_total
        hi, lo = split(block - average)
        at = pl.ds(pl.multiple_of(i * SIDE, SIDE), SIDE)
        anom[at, 0:128] = hi
        anom[at, 128:256] = lo
        mean_out[pl.ds(i, 1), :] = jnp.sum(jnp.where(eye, average, 0.0), axis=0, keepdims=True)
        return carry

    gy_begin()
    from_gy[gy] = parts[gy]
    lax.fori_loop(0, SIDE // 2, anomalies, 0, unroll=8)
    gy_end()
    held_y[...] = total(from_gy, n_gy)
    y_begin()
    from_y[y] = held_y[...]
    lax.fori_loop(SIDE // 2, SIDE, anomalies, 0, unroll=8)
    store = pltpu.make_async_copy(anom, anom_hbm, sem_anom)
    store.start()
    y_end()
    held_z[...] = total(from_y, ny)
    z_begin()
    from_z[z] = held_z[...]
    z_end()
    held_gy[...] = total(from_z, nz)
    back_begin()
    whole[gy] = held_gy[...]
    back_end()
    gram_out[...] = whole[...]
    store.wait()


def keep(array):
    return pltpu.with_memory_space_constraint(array, pltpu.HBM)


def forecast(nz, n_gx, n_gy, members, courant, cells, count, value, weight):
    ny = n_gx // nz
    piece = (128 // n_gy + 1, 128)
    f32 = jnp.float32
    state = pltpu.VMEM(((SIDE + 2) * PITCH, 128), f32)
    dma = pltpu.SemaphoreType.DMA
    vmem, smem, hbm, far = (
        pl.BlockSpec(memory_space=s) for s in (pltpu.VMEM, pltpu.SMEM, pl.ANY, pltpu.HBM)
    )
    return pl.pallas_call(
        functools.partial(forecast_kernel, nz, 128 * n_gx * n_gy),
        out_shape=(
            jax.ShapeDtypeStruct((n_gy,) + piece, f32),
            jax.ShapeDtypeStruct((SIDE * SIDE, 256), jnp.bfloat16),
            jax.ShapeDtypeStruct((SIDE, SIDE), f32),
        ),
        in_specs=[far, far, far, smem, far, far],
        out_specs=(vmem, hbm, vmem),
        scratch_shapes=[
            pltpu.VMEM((SIDE * SIDE, 128), jnp.bfloat16),
            pltpu.VMEM((2, SIDE, SIDE), f32),
            pltpu.SMEM((1, 128), jnp.int32),
            pltpu.VMEM((1, 128), f32),
            pltpu.VMEM((1, 128), f32),
            state, state, state, state,
            pltpu.VMEM((SIDE * SIDE, 128), f32),
            pltpu.VMEM((SIDE * SIDE, 128), f32),
            pltpu.VMEM((STEPS, 2, SIDE, 128), f32),
            pltpu.VMEM((STEPS, 2, SIDE, 128), f32),
            pltpu.VMEM((128, 128), f32),
            pltpu.VMEM((SIDE * SIDE, 256), jnp.bfloat16),
            pltpu.VMEM((n_gy,) + piece, f32),
            pltpu.VMEM((n_gy,) + piece, f32),
            pltpu.VMEM(piece, f32),
            pltpu.VMEM((ny,) + piece, f32),
            pltpu.VMEM(piece, f32),
            pltpu.VMEM((nz,) + piece, f32),
            pltpu.VMEM(piece, f32),
            pltpu.VMEM((n_gy,) + piece, f32),
            dma, dma((4,)), dma,
            dma((STEPS, 4)), dma((STEPS, 4)),
            dma((n_gy,)), dma((n_gy,)),
            dma((ny,)), dma((ny,)),
            dma((nz,)), dma((nz,)),
            dma((n_gy,)), dma((n_gy,)),
        ],
        compiler_params=pltpu.CompilerParams(
            collective_id=0, has_side_effects=True, vmem_limit_bytes=40 * 2**20
        ),
    )(keep(members), keep(courant), keep(cells), count, keep(value), keep(weight))


def shards(nz, n_gx, n_gy, members, courant, obs_cells, obs_count, obs_value, obs_weight):
    tile_rows, tile_cols, member_total = members.shape
    flat = members.reshape(tile_rows * tile_cols, member_total)
    gram, anom, mean = forecast(
        nz, n_gx, n_gy, flat, courant,
        obs_cells.reshape(1, -1), obs_count, obs_value.reshape(1, -1), obs_weight.reshape(1, -1),
    )
    out_mean, out_anom = transform(gram, anom, mean)
    return out_mean, out_anom.reshape(members.shape)


Z_CHIPS = 12


def solution(mesh):
    n_gx, n_gy = mesh.shape["gx"], mesh.shape["gy"]
    in_specs = (
        P("gx", "gy", None),
        P(None, "gx", "gy"),
        P("gx", "gy", None),
        P("gx", "gy"),
        P("gx", "gy", None),
        P("gx", "gy", None),
    )
    out_specs = (P("gx", "gy"), P("gx", "gy", None))
    body = functools.partial(shards, Z_CHIPS, n_gx, n_gy)
    return jax.shard_map(body, mesh=mesh, in_specs=in_specs, out_specs=out_specs, check_vma=False)
```

```python
import functools
import math

import jax
import jax.numpy as jnp
from jax import lax
from jax.experimental import pallas as pl
from jax.experimental.pallas import tpu as pltpu
from jax.sharding import PartitionSpec as P

M = 128
GROUPS = M // 8


def split(x):
    hi = x.astype(jnp.bfloat16)
    return hi, (x - hi.astype(jnp.float32)).astype(jnp.bfloat16)


def row_of(x, k):
    return jnp.broadcast_to(x[k : k + 1, :], x.shape)


def column_of(x, k):
    return jnp.broadcast_to(x[:, k : k + 1], (x.shape[0], 128))


def inverse_factor(gram_rows):
    sub = lax.broadcasted_iota(jnp.int32, (8, 128), 0)
    lane = lax.broadcasted_iota(jnp.int32, (8, 128), 1)
    a = [g + (lane == sub + 8 * i).astype(jnp.float32) for i, g in enumerate(gram_rows)]
    x = [(lane == sub + 8 * i).astype(jnp.float32) for i in range(GROUPS)]
    c = [column_of(a[0], j) for j in range(8)]
    for p in range(GROUPS):
        more = p + 1 < GROUPS
        if more:
            e = [column_of(a[p + 1], 8 * p + j) for j in range(8)]
            d = [column_of(a[p + 1], 8 * p + 8 + j) for j in range(8)]
        recip, upper, row_a, row_x = [], [], [], []
        pivots = jnp.ones((8, 128), jnp.float32)
        for k in range(8):
            pivot = row_of(c[k], k)
            r = 1.0 / pivot
            pivots = jnp.where(sub == k, pivot, pivots)
            recip.append(r)
            m = jnp.where(sub > k, c[k] * r, 0.0)
            upper.append([None] * 8)
            for j in range(k + 1, 8):
                upper[k][j] = row_of(c[j], k)
                c[j] = c[j] - m * upper[k][j]
            if more:
                n = e[k] * r
                for j in range(k + 1, 8):
                    e[j] = e[j] - n * upper[k][j]
                for j in range(8):
                    d[j] = d[j] - n * row_of(e[k], j)
            row_a.append(row_of(a[p], k))
            row_x.append(row_of(x[p], k))
            if k < 7:
                a[p] = a[p] - m * row_a[k]
                x[p] = x[p] - m * row_x[k]
            if more:
                a[p + 1] = a[p + 1] - n * row_a[k]
                x[p + 1] = x[p + 1] - n * row_x[k]
        for i in range(p + 2, GROUPS):
            f = [column_of(a[i], 8 * p + j) for j in range(8)]
            for k in range(8):
                m = f[k] * recip[k]
                for j in range(k + 1, 8):
                    f[j] = f[j] - m * upper[k][j]
                a[i] = a[i] - m * row_a[k]
                x[i] = x[i] - m * row_x[k]
        x[p] = x[p] * lax.rsqrt(pivots)
        if more:
            c = d
    return x


def transform_kernel(rows, gram_ref, anom_hbm, mean_ref, out_mean, out_hbm, anom, out, mix, flat, sem_in, sem_out):
    chunks = 4
    cells = anom.shape[0] // chunks
    load = pltpu.make_async_copy(anom_hbm, anom, sem_in)
    load.start()
    groups = []
    for i in range(GROUPS):
        piece, start = divmod(8 * i, rows)
        groups.append(gram_ref[piece, start : start + 8, :])
    x = inverse_factor(groups)
    cross = jnp.broadcast_to(gram_ref[0, rows : rows + 1, :], (8, 128))
    total = jnp.zeros((8, 128), jnp.float32)
    for i in range(GROUPS):
        y = jnp.sum(x[i] * cross, axis=1, keepdims=True)
        total = total + x[i] * y
    weights = jnp.broadcast_to(jnp.sum(total, axis=0, keepdims=True), (16, 128))
    for i in range(0, GROUPS, 2):
        hi, lo = split(jnp.concatenate([x[i], x[i + 1]], axis=0))
        mix[8 * i : 8 * i + 16, 0:128] = hi
        mix[8 * i : 8 * i + 16, 128:256] = hi
        mix[128 + 8 * i : 128 + 8 * i + 16, 0:128] = lo
        mix[128 + 8 * i : 128 + 8 * i + 16, 128:256] = jnp.zeros((16, 128), jnp.bfloat16)
    w_hi, w_lo = split(weights)
    w_both = jnp.concatenate([w_hi, w_hi], axis=1)
    w_low = jnp.concatenate([w_lo, jnp.zeros_like(w_lo)], axis=1)
    w_rows = jnp.concatenate([w_both, w_low], axis=0)
    load.wait()
    nt = (((1,), (1,)), ((), ()))
    for q in range(chunks):
        part = pl.ds(q * cells, cells)
        block = anom[part, :]
        both = lax.dot_general(block, mix[...], nt, preferred_element_type=jnp.float32)
        out[part, :] = (both[:, 0:128] + both[:, 128:256]).astype(jnp.bfloat16)
        pltpu.make_async_copy(out.at[part], out_hbm.at[part], sem_out.at[q]).start()
    for q in range(chunks):
        part = pl.ds(q * cells, cells)
        shift = lax.dot_general(w_rows, anom[part, :], nt, preferred_element_type=jnp.float32)
        line = shift[0:1, :] + shift[16:17, :]
        for i in range(cells // 128):
            n = q * (cells // 128) + i
            flat[n : n + 1, :] = line[:, 128 * i : 128 * i + 128]
    lines = flat[...]
    ny = out_mean.shape[1]
    half = flat.shape[0]
    even = lines[:, 0:ny]
    odd = pltpu.roll(lines, 128 - ny, axis=1)[:, 0:ny]
    out_mean[pl.ds(0, half, stride=2), :] = mean_ref[pl.ds(0, half, stride=2), :] + even
    out_mean[pl.ds(1, half, stride=2), :] = mean_ref[pl.ds(1, half, stride=2), :] + odd
    for q in range(chunks):
        part = pl.ds(q * cells, cells)
        pltpu.make_async_copy(out.at[part], out_hbm.at[part], sem_out.at[q]).wait()


def transform(gram, anom, mean):
    pieces, piece_rows, _ = gram.shape
    cells = anom.shape[0]
    return pl.pallas_call(
        functools.partial(transform_kernel, piece_rows - 1),
        out_shape=(
            jax.ShapeDtypeStruct(mean.shape, jnp.float32),
            jax.ShapeDtypeStruct((cells, M), jnp.bfloat16),
        ),
        in_specs=[
            pl.BlockSpec(memory_space=pltpu.VMEM),
            pl.BlockSpec(memory_space=pl.ANY),
            pl.BlockSpec(memory_space=pltpu.VMEM),
        ],
        out_specs=(pl.BlockSpec(memory_space=pltpu.VMEM), pl.BlockSpec(memory_space=pl.ANY)),
        scratch_shapes=[
            pltpu.VMEM((cells, 2 * M), jnp.bfloat16),
            pltpu.VMEM((cells, M), jnp.bfloat16),
            pltpu.VMEM((2 * M, 2 * M), jnp.bfloat16),
            pltpu.VMEM((cells // 128, 128), jnp.float32),
            pltpu.SemaphoreType.DMA,
            pltpu.SemaphoreType.DMA((4,)),
        ],
        compiler_params=pltpu.CompilerParams(vmem_limit_bytes=24 * 2**20),
    )(gram, anom, mean)


STEPS = 3
SIDE = 64
PITCH = 80
EDGE = 8
DIFFUSION = 0.2
HIGHEST = lax.Precision.HIGHEST
MESH = pl.DeviceIdType.MESH


def forecast_kernel(
    nz, total_slots,
    members_hbm, courant_hbm, cells_hbm, count_ref, value_hbm, weight_hbm,
    gram_out, anom_hbm, mean_out,
    members, courant_ref, cells_ref, value_ref, weight_ref, state0, state1, state2, state3, along, across, column_out, column_in,
    observed, anom, parts, from_gy, held_y, from_y, held_z, from_z, held_gy, whole,
    known, sem_members, sem_small, sem_anom, halo_send, halo_recv, gy_send, gy_recv, y_send, y_recv, z_send, z_recv, back_send, back_recv,
):
    states = [state0, state1, state2, state3]
    gx, gy = lax.axis_index("gx"), lax.axis_index("gy")
    n_gx, n_gy = lax.axis_size("gx"), lax.axis_size("gy")
    ny = n_gx // nz
    y, z = gx // nz, lax.rem(gx, nz)
    has_west, has_east, has_south, has_north = gx > 0, gx < n_gx - 1, gy > 0, gy < n_gy - 1

    load = pltpu.make_async_copy(members_hbm, members, sem_members)
    load.start()
    smalls = [
        pltpu.make_async_copy(source, target, sem_small.at[i])
        for i, (source, target) in enumerate(
            (
                (courant_hbm, courant_ref),
                (cells_hbm, cells_ref),
                (value_hbm, value_ref),
                (weight_hbm, weight_ref),
            )
        )
    ]
    for small in smalls:
        small.start()

    barrier = pltpu.get_barrier_semaphore()

    def greet(count, peer_of):
        def body(i, carry):
            pl.semaphore_signal(barrier, inc=1, device_id=peer_of(i), device_id_type=MESH)
            return carry
        lax.fori_loop(1, count, body, 0)

    def gy_peer(i):
        return lax.rem(gy + i, n_gy)

    def y_peer(i):
        return lax.rem(y + i, ny)

    def z_peer(i):
        return lax.rem(z + i, nz)

    def greet_ring(semaphore, distance, along_y):
        for shift in (distance, (ny if along_y else nz) - distance):
            target = y_peer(shift) * nz + z if along_y else y * nz + z_peer(shift)
            pl.semaphore_signal(semaphore, inc=1, device_id=(target, gy), device_id_type=MESH)

    greet(n_gy, lambda i: (gx, gy_peer(i)))
    greet_ring(barrier, 1, True)
    greet_ring(barrier, 1, False)
    far_west = jnp.logical_and(has_west, z == 0)
    far_east = jnp.logical_and(has_east, z == nz - 1)

    @pl.when(far_west)
    def _():
        pl.semaphore_signal(barrier, inc=1, device_id=(gx - 1, gy), device_id_type=MESH)

    @pl.when(far_east)
    def _():
        pl.semaphore_signal(barrier, inc=1, device_id=(gx + 1, gy), device_id_type=MESH)

    zeros = jnp.zeros((SIDE, 128), jnp.float32)
    low_row, high_row = pl.ds(EDGE, SIDE), pl.ds((SIDE + 1) * PITCH + EDGE, SIDE)
    first_row, last_row = pl.ds(PITCH + EDGE, SIDE), pl.ds(SIDE * PITCH + EDGE, SIDE)

    def column(cell, shift=0):
        return pl.ds((1 + shift) * PITCH + EDGE + cell, SIDE, stride=PITCH)

    for step in range(STEPS):
        @pl.when(jnp.logical_not(has_west))
        def _():
            states[step][low_row, :] = zeros

        @pl.when(jnp.logical_not(has_east))
        def _():
            states[step][high_row, :] = zeros

        @pl.when(jnp.logical_not(has_south))
        def _():
            column_in[step, 0] = zeros

        @pl.when(jnp.logical_not(has_north))
        def _():
            column_in[step, 1] = zeros

    load.wait()

    def rows_at(start, unit):
        return pl.ds(start if isinstance(start, int) else pl.multiple_of(start, unit), SIDE)

    def fill(i, carry):
        state0[rows_at((i + 1) * PITCH + EDGE, 8), :] = members[rows_at(i * SIDE, SIDE), :].astype(jnp.float32)
        return carry

    fill(0, 0)
    fill(SIDE - 1, 0)

    pl.semaphore_wait(
        barrier,
        (n_gy - 1) + 4 + far_west.astype(jnp.int32) + far_east.astype(jnp.int32),
    )

    there = (has_west, has_east, has_south, has_north)
    halo_devices = ((gx - 1, gy), (gx + 1, gy), (gx, gy - 1), (gx, gy + 1))

    def halo_copy(step, side):
        if side < 2:
            source = states[step].at[(first_row, last_row)[side]]
            target = states[step].at[(high_row, low_row)[side]]
        else:
            source, target = column_out.at[step, side - 2], column_in.at[step, 3 - side]
        return pltpu.make_async_remote_copy(
            src_ref=source, dst_ref=target,
            send_sem=halo_send.at[step, side], recv_sem=halo_recv.at[step, side ^ 1],
            device_id=halo_devices[side], device_id_type=MESH,
        )

    def start_halo(step, sides):
        for side in sides:
            @pl.when(there[side])
            def _():
                halo_copy(step, side).start()

    def finish_halo(step):
        for side in range(4):
            @pl.when(there[side])
            def _():
                halo_copy(step, side ^ 1).wait_recv()
                halo_copy(step, side).wait_send()

    start_halo(0, (0, 1))
    greet_ring(known.at[0], 1, True)
    greet_ring(known.at[1], 1, False)
    lax.fori_loop(1, SIDE - 1, fill, 0, unroll=2)
    column_out[0, 0] = state0[column(0), :]
    column_out[0, 1] = state0[column(SIDE - 1), :]
    start_halo(0, (2, 3))
    smalls[0].wait()

    eye_x = lax.broadcasted_iota(jnp.int32, (SIDE, SIDE), 0)
    eye_y = lax.broadcasted_iota(jnp.int32, (SIDE, SIDE), 1)
    eye = eye_x == eye_y

    def spread(i, carry):
        rows = pl.ds(pl.multiple_of(i * SIDE, SIDE), SIDE)
        for which, target in ((0, along), (1, across)):
            line = courant_ref[which, pl.ds(i, 1), :] * (0.5 / DIFFUSION)
            tall = jnp.sum(jnp.where(eye, line, 0.0), axis=1, keepdims=True)
            target[rows, :] = jnp.broadcast_to(tall, (SIDE, 128))
        return carry

    lax.fori_loop(0, SIDE, spread, 0, unroll=8)

    def update(state, at, flow_at):
        centre, east, west, north, south = (state[s, :] for s in at)
        return (
            ((east + west) + (north + south) + centre)
            - along[flow_at, :] * (east - west)
            - across[flow_at, :] * (north - south)
        )

    last_scale = DIFFUSION**STEPS

    def advance_row(step, i):
        base = rows_at((i + 1) * PITCH + EDGE, 8).start
        at = [pl.ds(base + s, SIDE) for s in (0, PITCH, -PITCH, 1, -1)]
        out = update(states[step], at, rows_at(i * SIDE, SIDE))
        if step == STEPS - 1:
            out = out * last_scale
        states[step + 1][at[0], :] = out

    def advance_column(step, cell):
        at = [column(cell), column(cell, 1), column(cell, -1), column(cell + 1), column(cell - 1)]
        return update(states[step], at, pl.ds(cell, SIDE, stride=SIDE))

    def place_columns(step):
        states[step][column(-1), :] = column_in[step, 0]
        states[step][column(SIDE), :] = column_in[step, 1]

    def advance_ends(step):
        place_columns(step)
        advance_row(step, 0)
        advance_row(step, SIDE - 1)

    def interior(step):
        def body(i, carry):
            advance_row(step, i)
            return carry
        lax.fori_loop(1, SIDE - 1, body, 0, unroll=2)

    for step in range(STEPS - 1):
        finish_halo(step)
        advance_ends(step)
        start_halo(step + 1, (0, 1))
        column_out[step + 1, 0] = advance_column(step, 0)
        column_out[step + 1, 1] = advance_column(step, SIDE - 1)
        start_halo(step + 1, (2, 3))
        if step == 0:
            pl.semaphore_wait(known.at[0], 2)
            pl.semaphore_wait(known.at[1], 2)
            greet_ring(known.at[2], 2, True)
            greet_ring(known.at[3], 2, False)
        if step == 1:
            pl.semaphore_wait(known.at[2], 2)
            pl.semaphore_wait(known.at[3], 2)
            greet_ring(known.at[4], 2, False)
        interior(step)

    final = STEPS - 1
    interior(final)
    finish_halo(final)
    advance_ends(final)
    for cell in (0, SIDE - 1):
        states[STEPS][column(cell), :] = advance_column(final, cell) * last_scale

    slots = observed.shape[0]

    def pick(s, carry):
        cell = cells_ref[0, s]
        row = (cell // SIDE + 1) * PITCH + EDGE + lax.rem(cell, SIDE)
        observed[pl.ds(s, 1), :] = state3[pl.ds(row, 1), :]
        return carry

    for small in smalls[1:]:
        small.wait()
    lax.fori_loop(0, slots, pick, 0, unroll=16)

    seen = observed[...].T
    members_total = seen.shape[0]
    seen_mean = jnp.sum(seen, axis=0, keepdims=True) / members_total
    live = lax.broadcasted_iota(jnp.int32, (1, slots), 1) < count_ref[0, 0]
    weight = weight_ref[...]
    scaled = (seen - seen_mean) * jnp.where(live, weight / math.sqrt(total_slots), 0.0)
    innovation = jnp.where(live, weight * (value_ref[...] - seen_mean), 0.0)
    left = jnp.concatenate([scaled, jnp.broadcast_to(innovation, (8, slots))], axis=0)
    nt = (((1,), (1,)), ((), ()))
    gram = lax.dot_general(left, scaled, nt, precision=HIGHEST, preferred_element_type=jnp.float32)
    rows = members_total // n_gy
    for j in range(n_gy):
        parts[j, 0:rows, :] = gram[j * rows : (j + 1) * rows, :]
        parts[j, rows : rows + 1, :] = gram[members_total : members_total + 1, :]

    def exchange(count, me, peer, device, source, target, send, recv):
        def copy(i, slot):
            return pltpu.make_async_remote_copy(
                src_ref=source(peer(i)), dst_ref=target.at[slot],
                send_sem=send.at[peer(i)], recv_sem=recv.at[slot],
                device_id=device(peer(i)), device_id_type=MESH,
            )

        def begin():
            def body(i, carry):
                copy(i, me).start()
                return carry
            lax.fori_loop(1, count, body, 0)

        def end():
            def body(i, carry):
                copy(i, peer(i)).wait_recv()
                copy(i, me).wait_send()
                return carry
            lax.fori_loop(1, count, body, 0)

        return begin, end

    def total(ref, count):
        out = ref[0]
        for j in range(1, count):
            out = out + ref[j]
        return out

    gy_begin, gy_end = exchange(
        n_gy, gy, gy_peer, lambda p: (gx, p), lambda p: parts.at[p], from_gy, gy_send, gy_recv
    )
    y_begin, y_end = exchange(
        ny, y, y_peer, lambda p: (p * nz + z, gy), lambda p: held_y, from_y, y_send, y_recv
    )
    z_begin, z_end = exchange(
        nz, z, z_peer, lambda p: (y * nz + p, gy), lambda p: held_z, from_z, z_send, z_recv
    )
    back_begin, back_end = exchange(
        n_gy, gy, gy_peer, lambda p: (gx, p), lambda p: held_gy, whole, back_send, back_recv
    )

    def anomalies(i, carry):
        block = state3[pl.ds(pl.multiple_of((i + 1) * PITCH + EDGE, 8), SIDE), :]
        average = jnp.sum(block, axis=1, keepdims=True) / members_total
        hi, lo = split(block - average)
        at = pl.ds(pl.multiple_of(i * SIDE, SIDE), SIDE)
        anom[at, 0:128] = hi
        anom[at, 128:256] = lo
        mean_out[pl.ds(i, 1), :] = jnp.sum(jnp.where(eye, average, 0.0), axis=0, keepdims=True)
        return carry

    gy_begin()
    from_gy[gy] = parts[gy]
    lax.fori_loop(0, SIDE // 2, anomalies, 0, unroll=8)
    gy_end()
    held_y[...] = total(from_gy, n_gy)
    y_begin()
    from_y[y] = held_y[...]
    lax.fori_loop(SIDE // 2, SIDE, anomalies, 0, unroll=8)
    store = pltpu.make_async_copy(anom, anom_hbm, sem_anom)
    store.start()
    y_end()
    held_z[...] = total(from_y, ny)
    pl.semaphore_wait(known.at[4], 2)
    z_begin()
    from_z[z] = held_z[...]
    z_end()
    held_gy[...] = total(from_z, nz)
    back_begin()
    whole[gy] = held_gy[...]
    back_end()
    gram_out[...] = whole[...]
    store.wait()


def keep(array):
    return pltpu.with_memory_space_constraint(array, pltpu.HBM)


def forecast(nz, n_gx, n_gy, members, courant, cells, count, value, weight):
    ny = n_gx // nz
    piece = (128 // n_gy + 1, 128)
    f32 = jnp.float32
    state = pltpu.VMEM(((SIDE + 2) * PITCH, 128), f32)
    dma = pltpu.SemaphoreType.DMA
    vmem, smem, hbm, far = (
        pl.BlockSpec(memory_space=s) for s in (pltpu.VMEM, pltpu.SMEM, pl.ANY, pltpu.HBM)
    )
    return pl.pallas_call(
        functools.partial(forecast_kernel, nz, 128 * n_gx * n_gy),
        out_shape=(
            jax.ShapeDtypeStruct((n_gy,) + piece, f32),
            jax.ShapeDtypeStruct((SIDE * SIDE, 256), jnp.bfloat16),
            jax.ShapeDtypeStruct((SIDE, SIDE), f32),
        ),
        in_specs=[far, far, far, smem, far, far],
        out_specs=(vmem, hbm, vmem),
        scratch_shapes=[
            pltpu.VMEM((SIDE * SIDE, 128), jnp.bfloat16),
            pltpu.VMEM((2, SIDE, SIDE), f32),
            pltpu.SMEM((1, 128), jnp.int32),
            pltpu.VMEM((1, 128), f32),
            pltpu.VMEM((1, 128), f32),
            state, state, state, state,
            pltpu.VMEM((SIDE * SIDE, 128), f32),
            pltpu.VMEM((SIDE * SIDE, 128), f32),
            pltpu.VMEM((STEPS, 2, SIDE, 128), f32),
            pltpu.VMEM((STEPS, 2, SIDE, 128), f32),
            pltpu.VMEM((128, 128), f32),
            pltpu.VMEM((SIDE * SIDE, 256), jnp.bfloat16),
            pltpu.VMEM((n_gy,) + piece, f32),
            pltpu.VMEM((n_gy,) + piece, f32),
            pltpu.VMEM(piece, f32),
            pltpu.VMEM((ny,) + piece, f32),
            pltpu.VMEM(piece, f32),
            pltpu.VMEM((nz,) + piece, f32),
            pltpu.VMEM(piece, f32),
            pltpu.VMEM((n_gy,) + piece, f32),
            pltpu.SemaphoreType.REGULAR((5,)),
            dma, dma((4,)), dma,
            dma((STEPS, 4)), dma((STEPS, 4)),
            dma((n_gy,)), dma((n_gy,)),
            dma((ny,)), dma((ny,)),
            dma((nz,)), dma((nz,)),
            dma((n_gy,)), dma((n_gy,)),
        ],
        compiler_params=pltpu.CompilerParams(
            collective_id=0, has_side_effects=True, vmem_limit_bytes=40 * 2**20
        ),
    )(keep(members), keep(courant), keep(cells), count, keep(value), keep(weight))


def shards(nz, n_gx, n_gy, members, courant, obs_cells, obs_count, obs_value, obs_weight):
    tile_rows, tile_cols, member_total = members.shape
    flat = members.reshape(tile_rows * tile_cols, member_total)
    gram, anom, mean = forecast(
        nz, n_gx, n_gy, flat, courant,
        obs_cells.reshape(1, -1), obs_count, obs_value.reshape(1, -1), obs_weight.reshape(1, -1),
    )
    out_mean, out_anom = transform(gram, anom, mean)
    return out_mean, out_anom.reshape(members.shape)


Z_CHIPS = 12


def solution(mesh):
    n_gx, n_gy = mesh.shape["gx"], mesh.shape["gy"]
    in_specs = (
        P("gx", "gy", None),
        P(None, "gx", "gy"),
        P("gx", "gy", None),
        P("gx", "gy"),
        P("gx", "gy", None),
        P("gx", "gy", None),
    )
    out_specs = (P("gx", "gy"), P("gx", "gy", None))
    body = functools.partial(shards, Z_CHIPS, n_gx, n_gy)
    return jax.shard_map(body, mesh=mesh, in_specs=in_specs, out_specs=out_specs, check_vma=False)
```

```python
import functools
import math

import jax
import jax.numpy as jnp
from jax import lax
from jax.experimental import pallas as pl
from jax.experimental.pallas import tpu as pltpu
from jax.sharding import PartitionSpec as P

M = 128
GROUPS = M // 8


def split(x):
    hi = x.astype(jnp.bfloat16)
    return hi, (x - hi.astype(jnp.float32)).astype(jnp.bfloat16)


def row_of(x, k):
    return jnp.broadcast_to(x[k : k + 1, :], x.shape)


def column_of(x, k):
    return jnp.broadcast_to(x[:, k : k + 1], (x.shape[0], 128))


def inverse_factor(gram_rows):
    sub = lax.broadcasted_iota(jnp.int32, (8, 128), 0)
    lane = lax.broadcasted_iota(jnp.int32, (8, 128), 1)
    a = [g + (lane == sub + 8 * i).astype(jnp.float32) for i, g in enumerate(gram_rows)]
    x = [(lane == sub + 8 * i).astype(jnp.float32) for i in range(GROUPS)]
    c = [column_of(a[0], j) for j in range(8)]
    for p in range(GROUPS):
        more = p + 1 < GROUPS
        if more:
            e = [column_of(a[p + 1], 8 * p + j) for j in range(8)]
            d = [column_of(a[p + 1], 8 * p + 8 + j) for j in range(8)]
        recip, upper, row_a, row_x = [], [], [], []
        pivots = jnp.ones((8, 128), jnp.float32)
        for k in range(8):
            pivot = row_of(c[k], k)
            r = 1.0 / pivot
            pivots = jnp.where(sub == k, pivot, pivots)
            recip.append(r)
            m = jnp.where(sub > k, c[k] * r, 0.0)
            upper.append([None] * 8)
            for j in range(k + 1, 8):
                upper[k][j] = row_of(c[j], k)
                c[j] = c[j] - m * upper[k][j]
            if more:
                n = e[k] * r
                for j in range(k + 1, 8):
                    e[j] = e[j] - n * upper[k][j]
                for j in range(8):
                    d[j] = d[j] - n * row_of(e[k], j)
            row_a.append(row_of(a[p], k))
            row_x.append(row_of(x[p], k))
            if k < 7:
                a[p] = a[p] - m * row_a[k]
                x[p] = x[p] - m * row_x[k]
            if more:
                a[p + 1] = a[p + 1] - n * row_a[k]
                x[p + 1] = x[p + 1] - n * row_x[k]
        for i in range(p + 2, GROUPS):
            f = [column_of(a[i], 8 * p + j) for j in range(8)]
            for k in range(8):
                m = f[k] * recip[k]
                for j in range(k + 1, 8):
                    f[j] = f[j] - m * upper[k][j]
                a[i] = a[i] - m * row_a[k]
                x[i] = x[i] - m * row_x[k]
        x[p] = x[p] * lax.rsqrt(pivots)
        if more:
            c = d
    return x


def transform_kernel(rows, gram_ref, anom_hbm, mean_ref, out_mean, out_hbm, anom, out, mix, flat, sem_in, sem_out):
    chunks = 4
    cells = anom.shape[0] // chunks
    load = pltpu.make_async_copy(anom_hbm, anom, sem_in)
    load.start()
    groups = []
    for i in range(GROUPS):
        piece, start = divmod(8 * i, rows)
        groups.append(gram_ref[piece, start : start + 8, :])
    x = inverse_factor(groups)
    cross = jnp.broadcast_to(gram_ref[0, rows : rows + 1, :], (8, 128))
    total = jnp.zeros((8, 128), jnp.float32)
    for i in range(GROUPS):
        y = jnp.sum(x[i] * cross, axis=1, keepdims=True)
        total = total + x[i] * y
    weights = jnp.broadcast_to(jnp.sum(total, axis=0, keepdims=True), (16, 128))
    for i in range(0, GROUPS, 2):
        hi, lo = split(jnp.concatenate([x[i], x[i + 1]], axis=0))
        mix[8 * i : 8 * i + 16, 0:128] = hi
        mix[8 * i : 8 * i + 16, 128:256] = hi
        mix[128 + 8 * i : 128 + 8 * i + 16, 0:128] = lo
        mix[128 + 8 * i : 128 + 8 * i + 16, 128:256] = jnp.zeros((16, 128), jnp.bfloat16)
    w_hi, w_lo = split(weights)
    w_both = jnp.concatenate([w_hi, w_hi], axis=1)
    w_low = jnp.concatenate([w_lo, jnp.zeros_like(w_lo)], axis=1)
    w_rows = jnp.concatenate([w_both, w_low], axis=0)
    load.wait()
    nt = (((1,), (1,)), ((), ()))
    for q in range(chunks):
        part = pl.ds(q * cells, cells)
        block = anom[part, :]
        both = lax.dot_general(block, mix[...], nt, preferred_element_type=jnp.float32)
        out[part, :] = (both[:, 0:128] + both[:, 128:256]).astype(jnp.bfloat16)
        pltpu.make_async_copy(out.at[part], out_hbm.at[part], sem_out.at[q]).start()
    for q in range(chunks):
        part = pl.ds(q * cells, cells)
        shift = lax.dot_general(w_rows, anom[part, :], nt, preferred_element_type=jnp.float32)
        line = shift[0:1, :] + shift[16:17, :]
        for i in range(cells // 128):
            n = q * (cells // 128) + i
            flat[n : n + 1, :] = line[:, 128 * i : 128 * i + 128]
    lines = flat[...]
    ny = out_mean.shape[1]
    half = flat.shape[0]
    even = lines[:, 0:ny]
    odd = pltpu.roll(lines, 128 - ny, axis=1)[:, 0:ny]
    out_mean[pl.ds(0, half, stride=2), :] = mean_ref[pl.ds(0, half, stride=2), :] + even
    out_mean[pl.ds(1, half, stride=2), :] = mean_ref[pl.ds(1, half, stride=2), :] + odd
    for q in range(chunks):
        part = pl.ds(q * cells, cells)
        pltpu.make_async_copy(out.at[part], out_hbm.at[part], sem_out.at[q]).wait()


def transform(gram, anom, mean):
    pieces, piece_rows, _ = gram.shape
    cells = anom.shape[0]
    return pl.pallas_call(
        functools.partial(transform_kernel, piece_rows - 1),
        out_shape=(
            jax.ShapeDtypeStruct(mean.shape, jnp.float32),
            jax.ShapeDtypeStruct((cells, M), jnp.bfloat16),
        ),
        in_specs=[
            pl.BlockSpec(memory_space=pltpu.VMEM),
            pl.BlockSpec(memory_space=pl.ANY),
            pl.BlockSpec(memory_space=pltpu.VMEM),
        ],
        out_specs=(pl.BlockSpec(memory_space=pltpu.VMEM), pl.BlockSpec(memory_space=pl.ANY)),
        scratch_shapes=[
            pltpu.VMEM((cells, 2 * M), jnp.bfloat16),
            pltpu.VMEM((cells, M), jnp.bfloat16),
            pltpu.VMEM((2 * M, 2 * M), jnp.bfloat16),
            pltpu.VMEM((cells // 128, 128), jnp.float32),
            pltpu.SemaphoreType.DMA,
            pltpu.SemaphoreType.DMA((4,)),
        ],
        compiler_params=pltpu.CompilerParams(vmem_limit_bytes=24 * 2**20),
    )(gram, anom, mean)


STEPS = 3
SIDE = 64
PITCH = 80
EDGE = 8
DIFFUSION = 0.2
HIGHEST = lax.Precision.HIGHEST
MESH = pl.DeviceIdType.MESH


def forecast_kernel(
    nz, total_slots,
    members_hbm, courant_hbm, cells_hbm, count_ref, value_hbm, weight_hbm,
    gram_out, anom_hbm, mean_out,
    members, courant_ref, cells_ref, value_ref, weight_ref, state0, state1, state2, state3, along, across, column_out, column_in,
    observed, anom, parts, from_gy, held_y, from_y, held_z, from_z, held_gy, whole,
    known, sem_members, sem_small, sem_anom, halo_send, halo_recv, gy_send, gy_recv, y_send, y_recv, z_send, z_recv, back_send, back_recv,
):
    states = [state0, state1, state2, state3]
    gx, gy = lax.axis_index("gx"), lax.axis_index("gy")
    n_gx, n_gy = lax.axis_size("gx"), lax.axis_size("gy")
    ny = n_gx // nz
    y, z = gx // nz, lax.rem(gx, nz)
    has_west, has_east, has_south, has_north = gx > 0, gx < n_gx - 1, gy > 0, gy < n_gy - 1

    load = pltpu.make_async_copy(members_hbm, members, sem_members)
    load.start()
    smalls = [
        pltpu.make_async_copy(source, target, sem_small.at[i])
        for i, (source, target) in enumerate(
            (
                (courant_hbm, courant_ref),
                (cells_hbm, cells_ref),
                (value_hbm, value_ref),
                (weight_hbm, weight_ref),
            )
        )
    ]
    for small in smalls:
        small.start()

    barrier = pltpu.get_barrier_semaphore()

    def gy_peer(i):
        return lax.rem(gy + i, n_gy)

    def y_peer(i):
        return lax.rem(y + i, ny)

    def z_peer(i):
        return lax.rem(z + i, nz)

    rings = {
        "gy": (n_gy, lambda i: (gx, gy_peer(i))),
        "y": (ny, lambda i: (y_peer(i) * nz + z, gy)),
        "z": (nz, lambda i: (y * nz + z_peer(i), gy)),
    }

    def greet_ring(ring, semaphore, distance):
        count, device = rings[ring]
        for shift in (distance, count - distance):
            pl.semaphore_signal(semaphore, inc=1, device_id=device(shift), device_id_type=MESH)

    for ring in rings:
        greet_ring(ring, barrier, 1)
    far_west = jnp.logical_and(has_west, z == 0)
    far_east = jnp.logical_and(has_east, z == nz - 1)

    @pl.when(far_west)
    def _():
        pl.semaphore_signal(barrier, inc=1, device_id=(gx - 1, gy), device_id_type=MESH)

    @pl.when(far_east)
    def _():
        pl.semaphore_signal(barrier, inc=1, device_id=(gx + 1, gy), device_id_type=MESH)

    zeros = jnp.zeros((SIDE, 128), jnp.float32)
    low_row, high_row = pl.ds(EDGE, SIDE), pl.ds((SIDE + 1) * PITCH + EDGE, SIDE)
    first_row, last_row = pl.ds(PITCH + EDGE, SIDE), pl.ds(SIDE * PITCH + EDGE, SIDE)

    def column(cell, shift=0):
        return pl.ds((1 + shift) * PITCH + EDGE + cell, SIDE, stride=PITCH)

    for step in range(STEPS):
        @pl.when(jnp.logical_not(has_west))
        def _():
            states[step][low_row, :] = zeros

        @pl.when(jnp.logical_not(has_east))
        def _():
            states[step][high_row, :] = zeros

        @pl.when(jnp.logical_not(has_south))
        def _():
            column_in[step, 0] = zeros

        @pl.when(jnp.logical_not(has_north))
        def _():
            column_in[step, 1] = zeros

    load.wait()

    def rows_at(start, unit):
        return pl.ds(start if isinstance(start, int) else pl.multiple_of(start, unit), SIDE)

    def fill(i, carry):
        state0[rows_at((i + 1) * PITCH + EDGE, 8), :] = members[rows_at(i * SIDE, SIDE), :].astype(jnp.float32)
        return carry

    fill(0, 0)
    fill(SIDE - 1, 0)

    pl.semaphore_wait(
        barrier,
        6 + far_west.astype(jnp.int32) + far_east.astype(jnp.int32),
    )

    there = (has_west, has_east, has_south, has_north)
    halo_devices = ((gx - 1, gy), (gx + 1, gy), (gx, gy - 1), (gx, gy + 1))

    def halo_copy(step, side):
        if side < 2:
            source = states[step].at[(first_row, last_row)[side]]
            target = states[step].at[(high_row, low_row)[side]]
        else:
            source, target = column_out.at[step, side - 2], column_in.at[step, 3 - side]
        return pltpu.make_async_remote_copy(
            src_ref=source, dst_ref=target,
            send_sem=halo_send.at[step, side], recv_sem=halo_recv.at[step, side ^ 1],
            device_id=halo_devices[side], device_id_type=MESH,
        )

    def start_halo(step, sides):
        for side in sides:
            @pl.when(there[side])
            def _():
                halo_copy(step, side).start()

    def finish_halo(step):
        for side in range(4):
            @pl.when(there[side])
            def _():
                halo_copy(step, side ^ 1).wait_recv()
                halo_copy(step, side).wait_send()

    start_halo(0, (0, 1))
    for i, ring in enumerate(rings):
        greet_ring(ring, known.at[0, i], 1)
    lax.fori_loop(1, SIDE - 1, fill, 0, unroll=2)
    column_out[0, 0] = state0[column(0), :]
    column_out[0, 1] = state0[column(SIDE - 1), :]
    start_halo(0, (2, 3))
    smalls[0].wait()

    eye_x = lax.broadcasted_iota(jnp.int32, (SIDE, SIDE), 0)
    eye_y = lax.broadcasted_iota(jnp.int32, (SIDE, SIDE), 1)
    eye = eye_x == eye_y

    def spread(i, carry):
        rows = pl.ds(pl.multiple_of(i * SIDE, SIDE), SIDE)
        for which, target in ((0, along), (1, across)):
            line = courant_ref[which, pl.ds(i, 1), :] * (0.5 / DIFFUSION)
            tall = jnp.sum(jnp.where(eye, line, 0.0), axis=1, keepdims=True)
            target[rows, :] = jnp.broadcast_to(tall, (SIDE, 128))
        return carry

    lax.fori_loop(0, SIDE, spread, 0, unroll=8)

    def update(state, at, flow_at):
        centre, east, west, north, south = (state[s, :] for s in at)
        return (
            ((east + west) + (north + south) + centre)
            - along[flow_at, :] * (east - west)
            - across[flow_at, :] * (north - south)
        )

    last_scale = DIFFUSION**STEPS

    def advance_row(step, i):
        base = rows_at((i + 1) * PITCH + EDGE, 8).start
        at = [pl.ds(base + s, SIDE) for s in (0, PITCH, -PITCH, 1, -1)]
        out = update(states[step], at, rows_at(i * SIDE, SIDE))
        if step == STEPS - 1:
            out = out * last_scale
        states[step + 1][at[0], :] = out

    def advance_column(step, cell):
        at = [column(cell), column(cell, 1), column(cell, -1), column(cell + 1), column(cell - 1)]
        return update(states[step], at, pl.ds(cell, SIDE, stride=SIDE))

    def place_columns(step):
        states[step][column(-1), :] = column_in[step, 0]
        states[step][column(SIDE), :] = column_in[step, 1]

    def advance_ends(step):
        place_columns(step)
        advance_row(step, 0)
        advance_row(step, SIDE - 1)

    def interior(step):
        def body(i, carry):
            advance_row(step, i)
            return carry
        lax.fori_loop(1, SIDE - 1, body, 0, unroll=2)

    for step in range(STEPS - 1):
        finish_halo(step)
        advance_ends(step)
        start_halo(step + 1, (0, 1))
        column_out[step + 1, 0] = advance_column(step, 0)
        column_out[step + 1, 1] = advance_column(step, SIDE - 1)
        start_halo(step + 1, (2, 3))
        if step == 0:
            for i, ring in enumerate(rings):
                pl.semaphore_wait(known.at[0, i], 2)
                greet_ring(ring, known.at[1, i], 2)
        if step == 1:
            for i in range(len(rings)):
                pl.semaphore_wait(known.at[1, i], 2)
            greet_ring("z", known.at[2, 2], 2)
        interior(step)

    final = STEPS - 1
    interior(final)
    finish_halo(final)
    advance_ends(final)
    for cell in (0, SIDE - 1):
        states[STEPS][column(cell), :] = advance_column(final, cell) * last_scale

    slots = observed.shape[0]

    def pick(s, carry):
        cell = cells_ref[0, s]
        row = (cell // SIDE + 1) * PITCH + EDGE + lax.rem(cell, SIDE)
        observed[pl.ds(s, 1), :] = state3[pl.ds(row, 1), :]
        return carry

    for small in smalls[1:]:
        small.wait()
    lax.fori_loop(0, slots, pick, 0, unroll=16)

    seen = observed[...].T
    members_total = seen.shape[0]
    seen_mean = jnp.sum(seen, axis=0, keepdims=True) / members_total
    live = lax.broadcasted_iota(jnp.int32, (1, slots), 1) < count_ref[0, 0]
    weight = weight_ref[...]
    scaled = (seen - seen_mean) * jnp.where(live, weight / math.sqrt(total_slots), 0.0)
    innovation = jnp.where(live, weight * (value_ref[...] - seen_mean), 0.0)
    left = jnp.concatenate([scaled, jnp.broadcast_to(innovation, (8, slots))], axis=0)
    nt = (((1,), (1,)), ((), ()))
    gram = lax.dot_general(left, scaled, nt, precision=HIGHEST, preferred_element_type=jnp.float32)
    rows = members_total // n_gy
    for j in range(n_gy):
        parts[j, 0:rows, :] = gram[j * rows : (j + 1) * rows, :]
        parts[j, rows : rows + 1, :] = gram[members_total : members_total + 1, :]

    def exchange(count, me, peer, device, source, target, send, recv):
        def copy(i, slot):
            return pltpu.make_async_remote_copy(
                src_ref=source(peer(i)), dst_ref=target.at[slot],
                send_sem=send.at[peer(i)], recv_sem=recv.at[slot],
                device_id=device(peer(i)), device_id_type=MESH,
            )

        def begin():
            def body(i, carry):
                half = (i + 1) // 2
                copy(count // 2 + half * (1 - 2 * lax.rem(i, 2)), me).start()
                return carry
            lax.fori_loop(0, count - 1, body, 0)

        def end():
            def body(i, carry):
                copy(i, peer(i)).wait_recv()
                copy(i, me).wait_send()
                return carry
            lax.fori_loop(1, count, body, 0)

        return begin, end

    def total(ref, count):
        out = ref[0]
        for j in range(1, count):
            out = out + ref[j]
        return out

    gy_begin, gy_end = exchange(
        n_gy, gy, gy_peer, lambda p: (gx, p), lambda p: parts.at[p], from_gy, gy_send, gy_recv
    )
    y_begin, y_end = exchange(
        ny, y, y_peer, lambda p: (p * nz + z, gy), lambda p: held_y, from_y, y_send, y_recv
    )
    z_begin, z_end = exchange(
        nz, z, z_peer, lambda p: (y * nz + p, gy), lambda p: held_z, from_z, z_send, z_recv
    )
    back_begin, back_end = exchange(
        n_gy, gy, gy_peer, lambda p: (gx, p), lambda p: held_gy, whole, back_send, back_recv
    )

    def anomalies(i, carry):
        block = state3[pl.ds(pl.multiple_of((i + 1) * PITCH + EDGE, 8), SIDE), :]
        average = jnp.sum(block, axis=1, keepdims=True) / members_total
        hi, lo = split(block - average)
        at = pl.ds(pl.multiple_of(i * SIDE, SIDE), SIDE)
        anom[at, 0:128] = hi
        anom[at, 128:256] = lo
        mean_out[pl.ds(i, 1), :] = jnp.sum(jnp.where(eye, average, 0.0), axis=0, keepdims=True)
        return carry

    gy_begin()
    from_gy[gy] = parts[gy]
    lax.fori_loop(0, SIDE // 2, anomalies, 0, unroll=8)
    gy_end()
    held_y[...] = total(from_gy, n_gy)
    y_begin()
    from_y[y] = held_y[...]
    lax.fori_loop(SIDE // 2, SIDE, anomalies, 0, unroll=8)
    store = pltpu.make_async_copy(anom, anom_hbm, sem_anom)
    store.start()
    y_end()
    held_z[...] = total(from_y, ny)
    pl.semaphore_wait(known.at[2, 2], 2)
    z_begin()
    from_z[z] = held_z[...]
    z_end()
    held_gy[...] = total(from_z, nz)
    back_begin()
    whole[gy] = held_gy[...]
    back_end()
    gram_out[...] = whole[...]
    store.wait()


def keep(array):
    return pltpu.with_memory_space_constraint(array, pltpu.HBM)


def forecast(nz, n_gx, n_gy, members, courant, cells, count, value, weight):
    ny = n_gx // nz
    piece = (128 // n_gy + 1, 128)
    f32 = jnp.float32
    state = pltpu.VMEM(((SIDE + 2) * PITCH, 128), f32)
    dma = pltpu.SemaphoreType.DMA
    vmem, smem, hbm, far = (
        pl.BlockSpec(memory_space=s) for s in (pltpu.VMEM, pltpu.SMEM, pl.ANY, pltpu.HBM)
    )
    return pl.pallas_call(
        functools.partial(forecast_kernel, nz, 128 * n_gx * n_gy),
        out_shape=(
            jax.ShapeDtypeStruct((n_gy,) + piece, f32),
            jax.ShapeDtypeStruct((SIDE * SIDE, 256), jnp.bfloat16),
            jax.ShapeDtypeStruct((SIDE, SIDE), f32),
        ),
        in_specs=[far, far, far, smem, far, far],
        out_specs=(vmem, hbm, vmem),
        scratch_shapes=[
            pltpu.VMEM((SIDE * SIDE, 128), jnp.bfloat16),
            pltpu.VMEM((2, SIDE, SIDE), f32),
            pltpu.SMEM((1, 128), jnp.int32),
            pltpu.VMEM((1, 128), f32),
            pltpu.VMEM((1, 128), f32),
            state, state, state, state,
            pltpu.VMEM((SIDE * SIDE, 128), f32),
            pltpu.VMEM((SIDE * SIDE, 128), f32),
            pltpu.VMEM((STEPS, 2, SIDE, 128), f32),
            pltpu.VMEM((STEPS, 2, SIDE, 128), f32),
            pltpu.VMEM((128, 128), f32),
            pltpu.VMEM((SIDE * SIDE, 256), jnp.bfloat16),
            pltpu.VMEM((n_gy,) + piece, f32),
            pltpu.VMEM((n_gy,) + piece, f32),
            pltpu.VMEM(piece, f32),
            pltpu.VMEM((ny,) + piece, f32),
            pltpu.VMEM(piece, f32),
            pltpu.VMEM((nz,) + piece, f32),
            pltpu.VMEM(piece, f32),
            pltpu.VMEM((n_gy,) + piece, f32),
            pltpu.SemaphoreType.REGULAR((3, 3)),
            dma, dma((4,)), dma,
            dma((STEPS, 4)), dma((STEPS, 4)),
            dma((n_gy,)), dma((n_gy,)),
            dma((ny,)), dma((ny,)),
            dma((nz,)), dma((nz,)),
            dma((n_gy,)), dma((n_gy,)),
        ],
        compiler_params=pltpu.CompilerParams(
            collective_id=0, has_side_effects=True, vmem_limit_bytes=40 * 2**20
        ),
    )(keep(members), keep(courant), keep(cells), count, keep(value), keep(weight))


def shards(nz, n_gx, n_gy, members, courant, obs_cells, obs_count, obs_value, obs_weight):
    tile_rows, tile_cols, member_total = members.shape
    flat = members.reshape(tile_rows * tile_cols, member_total)
    gram, anom, mean = forecast(
        nz, n_gx, n_gy, flat, courant,
        obs_cells.reshape(1, -1), obs_count, obs_value.reshape(1, -1), obs_weight.reshape(1, -1),
    )
    out_mean, out_anom = transform(gram, anom, mean)
    return out_mean, out_anom.reshape(members.shape)


Z_CHIPS = 12


def solution(mesh):
    n_gx, n_gy = mesh.shape["gx"], mesh.shape["gy"]
    in_specs = (
        P("gx", "gy", None),
        P(None, "gx", "gy"),
        P("gx", "gy", None),
        P("gx", "gy"),
        P("gx", "gy", None),
        P("gx", "gy", None),
    )
    out_specs = (P("gx", "gy"), P("gx", "gy", None))
    body = functools.partial(shards, Z_CHIPS, n_gx, n_gy)
    return jax.shard_map(body, mesh=mesh, in_specs=in_specs, out_specs=out_specs, check_vma=False)
```

```python
import functools
import math

import jax
import jax.numpy as jnp
from jax import lax
from jax.experimental import pallas as pl
from jax.experimental.pallas import tpu as pltpu
from jax.sharding import PartitionSpec as P

M = 128
GROUPS = M // 8


def split(x):
    hi = x.astype(jnp.bfloat16)
    return hi, (x - hi.astype(jnp.float32)).astype(jnp.bfloat16)


def row_of(x, k):
    return jnp.broadcast_to(x[k : k + 1, :], x.shape)


def column_of(x, k):
    return jnp.broadcast_to(x[:, k : k + 1], (x.shape[0], 128))


def inverse_factor(gram_rows):
    sub = lax.broadcasted_iota(jnp.int32, (8, 128), 0)
    lane = lax.broadcasted_iota(jnp.int32, (8, 128), 1)
    a = [g + (lane == sub + 8 * i).astype(jnp.float32) for i, g in enumerate(gram_rows)]
    x = [(lane == sub + 8 * i).astype(jnp.float32) for i in range(GROUPS)]
    c = [column_of(a[0], j) for j in range(8)]
    for p in range(GROUPS):
        more = p + 1 < GROUPS
        if more:
            e = [column_of(a[p + 1], 8 * p + j) for j in range(8)]
            d = [column_of(a[p + 1], 8 * p + 8 + j) for j in range(8)]
        recip, upper, row_a, row_x = [], [], [], []
        pivots = jnp.ones((8, 128), jnp.float32)
        for k in range(8):
            pivot = row_of(c[k], k)
            r = 1.0 / pivot
            pivots = jnp.where(sub == k, pivot, pivots)
            recip.append(r)
            m = jnp.where(sub > k, c[k] * r, 0.0)
            upper.append([None] * 8)
            for j in range(k + 1, 8):
                upper[k][j] = row_of(c[j], k)
                c[j] = c[j] - m * upper[k][j]
            if more:
                n = e[k] * r
                for j in range(k + 1, 8):
                    e[j] = e[j] - n * upper[k][j]
                for j in range(8):
                    d[j] = d[j] - n * row_of(e[k], j)
            row_a.append(row_of(a[p], k))
            row_x.append(row_of(x[p], k))
            if k < 7:
                a[p] = a[p] - m * row_a[k]
                x[p] = x[p] - m * row_x[k]
            if more:
                a[p + 1] = a[p + 1] - n * row_a[k]
                x[p + 1] = x[p + 1] - n * row_x[k]
        for i in range(p + 2, GROUPS):
            f = [column_of(a[i], 8 * p + j) for j in range(8)]
            for k in range(8):
                m = f[k] * recip[k]
                for j in range(k + 1, 8):
                    f[j] = f[j] - m * upper[k][j]
                a[i] = a[i] - m * row_a[k]
                x[i] = x[i] - m * row_x[k]
        x[p] = x[p] * lax.rsqrt(pivots)
        if more:
            c = d
    return x


def transform_kernel(rows, gram_ref, anom_hbm, mean_ref, out_mean, out_hbm, anom, out, mix, flat, sem_in, sem_out):
    chunks = 4
    cells = anom.shape[0] // chunks
    load = pltpu.make_async_copy(anom_hbm, anom, sem_in)
    load.start()
    groups = []
    for i in range(GROUPS):
        piece, start = divmod(8 * i, rows)
        groups.append(gram_ref[piece, start : start + 8, :])
    x = inverse_factor(groups)
    cross = jnp.broadcast_to(gram_ref[0, rows : rows + 1, :], (8, 128))
    total = jnp.zeros((8, 128), jnp.float32)
    for i in range(GROUPS):
        y = jnp.sum(x[i] * cross, axis=1, keepdims=True)
        total = total + x[i] * y
    weights = jnp.broadcast_to(jnp.sum(total, axis=0, keepdims=True), (16, 128))
    for i in range(0, GROUPS, 2):
        hi, lo = split(jnp.concatenate([x[i], x[i + 1]], axis=0))
        mix[8 * i : 8 * i + 16, 0:128] = hi
        mix[8 * i : 8 * i + 16, 128:256] = hi
        mix[128 + 8 * i : 128 + 8 * i + 16, 0:128] = lo
        mix[128 + 8 * i : 128 + 8 * i + 16, 128:256] = jnp.zeros((16, 128), jnp.bfloat16)
    w_hi, w_lo = split(weights)
    w_both = jnp.concatenate([w_hi, w_hi], axis=1)
    w_low = jnp.concatenate([w_lo, jnp.zeros_like(w_lo)], axis=1)
    w_rows = jnp.concatenate([w_both, w_low], axis=0)
    load.wait()
    nt = (((1,), (1,)), ((), ()))
    for q in range(chunks):
        part = pl.ds(q * cells, cells)
        block = anom[part, :]
        both = lax.dot_general(block, mix[...], nt, preferred_element_type=jnp.float32)
        out[part, :] = (both[:, 0:128] + both[:, 128:256]).astype(jnp.bfloat16)
        pltpu.make_async_copy(out.at[part], out_hbm.at[part], sem_out.at[q]).start()
    for q in range(chunks):
        part = pl.ds(q * cells, cells)
        shift = lax.dot_general(w_rows, anom[part, :], nt, preferred_element_type=jnp.float32)
        line = shift[0:1, :] + shift[16:17, :]
        for i in range(cells // 128):
            n = q * (cells // 128) + i
            flat[n : n + 1, :] = line[:, 128 * i : 128 * i + 128]
    lines = flat[...]
    ny = out_mean.shape[1]
    half = flat.shape[0]
    even = lines[:, 0:ny]
    odd = pltpu.roll(lines, 128 - ny, axis=1)[:, 0:ny]
    out_mean[pl.ds(0, half, stride=2), :] = mean_ref[pl.ds(0, half, stride=2), :] + even
    out_mean[pl.ds(1, half, stride=2), :] = mean_ref[pl.ds(1, half, stride=2), :] + odd
    for q in range(chunks):
        part = pl.ds(q * cells, cells)
        pltpu.make_async_copy(out.at[part], out_hbm.at[part], sem_out.at[q]).wait()


def transform(gram, anom, mean):
    pieces, piece_rows, _ = gram.shape
    cells = anom.shape[0]
    return pl.pallas_call(
        functools.partial(transform_kernel, piece_rows - 1),
        out_shape=(
            jax.ShapeDtypeStruct(mean.shape, jnp.float32),
            jax.ShapeDtypeStruct((cells, M), jnp.bfloat16),
        ),
        in_specs=[
            pl.BlockSpec(memory_space=pltpu.VMEM),
            pl.BlockSpec(memory_space=pl.ANY),
            pl.BlockSpec(memory_space=pltpu.VMEM),
        ],
        out_specs=(pl.BlockSpec(memory_space=pltpu.VMEM), pl.BlockSpec(memory_space=pl.ANY)),
        scratch_shapes=[
            pltpu.VMEM((cells, 2 * M), jnp.bfloat16),
            pltpu.VMEM((cells, M), jnp.bfloat16),
            pltpu.VMEM((2 * M, 2 * M), jnp.bfloat16),
            pltpu.VMEM((cells // 128, 128), jnp.float32),
            pltpu.SemaphoreType.DMA,
            pltpu.SemaphoreType.DMA((4,)),
        ],
        compiler_params=pltpu.CompilerParams(vmem_limit_bytes=24 * 2**20),
    )(gram, anom, mean)


STEPS = 3
SIDE = 64
PITCH = 80
EDGE = 8
DIFFUSION = 0.2
HIGHEST = lax.Precision.HIGHEST
MESH = pl.DeviceIdType.MESH


def forecast_kernel(
    nz, total_slots,
    members_hbm, courant_hbm, cells_hbm, count_ref, value_hbm, weight_hbm,
    gram_out, anom_hbm, mean_out,
    members, courant_ref, cells_ref, value_ref, weight_ref, state0, state1, state2, state3, along, across, column_out, column_in,
    observed, anom, parts, from_gy, held_y, from_y, held_z, from_z, held_gy, whole,
    known, sem_members, sem_small, sem_anom, halo_send, halo_recv, gy_send, gy_recv, y_send, y_recv, z_send, z_recv, back_send, back_recv,
):
    states = [state0, state1, state2, state3]
    gx, gy = lax.axis_index("gx"), lax.axis_index("gy")
    n_gx, n_gy = lax.axis_size("gx"), lax.axis_size("gy")
    ny = n_gx // nz
    y, z = gx // nz, lax.rem(gx, nz)
    has_west, has_east, has_south, has_north = gx > 0, gx < n_gx - 1, gy > 0, gy < n_gy - 1

    load = pltpu.make_async_copy(members_hbm, members, sem_members)
    load.start()
    smalls = [
        pltpu.make_async_copy(source, target, sem_small.at[i])
        for i, (source, target) in enumerate(
            (
                (courant_hbm, courant_ref),
                (cells_hbm, cells_ref),
                (value_hbm, value_ref),
                (weight_hbm, weight_ref),
            )
        )
    ]
    for small in smalls:
        small.start()

    barrier = pltpu.get_barrier_semaphore()

    def gy_peer(i):
        return lax.rem(gy + i, n_gy)

    def y_peer(i):
        return lax.rem(y + i, ny)

    def z_peer(i):
        return lax.rem(z + i, nz)

    rings = {
        "gy": (n_gy, lambda i: (gx, gy_peer(i))),
        "y": (ny, lambda i: (y_peer(i) * nz + z, gy)),
        "z": (nz, lambda i: (y * nz + z_peer(i), gy)),
    }

    def greet_ring(ring, semaphore, distance):
        count, device = rings[ring]
        for shift in (distance, count - distance):
            pl.semaphore_signal(semaphore, inc=1, device_id=device(shift), device_id_type=MESH)

    for ring in rings:
        greet_ring(ring, barrier, 1)
    far_west = jnp.logical_and(has_west, z == 0)
    far_east = jnp.logical_and(has_east, z == nz - 1)

    @pl.when(far_west)
    def _():
        pl.semaphore_signal(barrier, inc=1, device_id=(gx - 1, gy), device_id_type=MESH)

    @pl.when(far_east)
    def _():
        pl.semaphore_signal(barrier, inc=1, device_id=(gx + 1, gy), device_id_type=MESH)

    zeros = jnp.zeros((SIDE, 128), jnp.float32)
    low_row, high_row = pl.ds(EDGE, SIDE), pl.ds((SIDE + 1) * PITCH + EDGE, SIDE)
    first_row, last_row = pl.ds(PITCH + EDGE, SIDE), pl.ds(SIDE * PITCH + EDGE, SIDE)

    def column(cell, shift=0):
        return pl.ds((1 + shift) * PITCH + EDGE + cell, SIDE, stride=PITCH)

    for step in range(STEPS):
        @pl.when(jnp.logical_not(has_west))
        def _():
            states[step][low_row, :] = zeros

        @pl.when(jnp.logical_not(has_east))
        def _():
            states[step][high_row, :] = zeros

        @pl.when(jnp.logical_not(has_south))
        def _():
            column_in[step, 0] = zeros

        @pl.when(jnp.logical_not(has_north))
        def _():
            column_in[step, 1] = zeros

    load.wait()

    def rows_at(start, unit):
        return pl.ds(start if isinstance(start, int) else pl.multiple_of(start, unit), SIDE)

    def fill(i, carry):
        state0[rows_at((i + 1) * PITCH + EDGE, 8), :] = members[rows_at(i * SIDE, SIDE), :].astype(jnp.float32)
        return carry

    fill(0, 0)
    fill(SIDE - 1, 0)

    pl.semaphore_wait(
        barrier,
        6 + far_west.astype(jnp.int32) + far_east.astype(jnp.int32),
    )

    there = (has_west, has_east, has_south, has_north)
    halo_devices = ((gx - 1, gy), (gx + 1, gy), (gx, gy - 1), (gx, gy + 1))

    def halo_copy(step, side):
        if side < 2:
            source = states[step].at[(first_row, last_row)[side]]
            target = states[step].at[(high_row, low_row)[side]]
        else:
            source, target = column_out.at[step, side - 2], column_in.at[step, 3 - side]
        return pltpu.make_async_remote_copy(
            src_ref=source, dst_ref=target,
            send_sem=halo_send.at[step, side], recv_sem=halo_recv.at[step, side ^ 1],
            device_id=halo_devices[side], device_id_type=MESH,
        )

    def start_halo(step, sides):
        for side in sides:
            @pl.when(there[side])
            def _():
                halo_copy(step, side).start()

    def await_halo(step, sides):
        for side in sides:
            @pl.when(there[side])
            def _():
                halo_copy(step, side ^ 1).wait_recv()

    def await_sent(step):
        for side in range(4):
            @pl.when(there[side])
            def _():
                halo_copy(step, side).wait_send()

    start_halo(0, (0, 1))
    for i, ring in enumerate(rings):
        greet_ring(ring, known.at[0, i], 1)
    lax.fori_loop(1, SIDE - 1, fill, 0, unroll=2)
    column_out[0, 0] = state0[column(0), :]
    column_out[0, 1] = state0[column(SIDE - 1), :]
    start_halo(0, (2, 3))
    smalls[0].wait()

    eye_x = lax.broadcasted_iota(jnp.int32, (SIDE, SIDE), 0)
    eye_y = lax.broadcasted_iota(jnp.int32, (SIDE, SIDE), 1)
    eye = eye_x == eye_y

    def spread(i, carry):
        rows = pl.ds(pl.multiple_of(i * SIDE, SIDE), SIDE)
        for which, target in ((0, along), (1, across)):
            line = courant_ref[which, pl.ds(i, 1), :] * (0.5 / DIFFUSION)
            tall = jnp.sum(jnp.where(eye, line, 0.0), axis=1, keepdims=True)
            target[rows, :] = jnp.broadcast_to(tall, (SIDE, 128))
        return carry

    lax.fori_loop(0, SIDE, spread, 0, unroll=8)

    def update(state, at, flow_at):
        centre, east, west, north, south = (state[s, :] for s in at)
        return (
            ((east + west) + (north + south) + centre)
            - along[flow_at, :] * (east - west)
            - across[flow_at, :] * (north - south)
        )

    last_scale = DIFFUSION**STEPS

    def advance_row(step, i):
        base = rows_at((i + 1) * PITCH + EDGE, 8).start
        at = [pl.ds(base + s, SIDE) for s in (0, PITCH, -PITCH, 1, -1)]
        out = update(states[step], at, rows_at(i * SIDE, SIDE))
        if step == STEPS - 1:
            out = out * last_scale
        states[step + 1][at[0], :] = out

    def advance_column(step, cell):
        at = [column(cell), column(cell, 1), column(cell, -1), column(cell + 1), column(cell - 1)]
        return update(states[step], at, pl.ds(cell, SIDE, stride=SIDE))

    def place_columns(step):
        states[step][column(-1), :] = column_in[step, 0]
        states[step][column(SIDE), :] = column_in[step, 1]

    def advance_ends(step):
        await_halo(step, (2, 3))
        place_columns(step)
        await_halo(step, (0, 1))
        advance_row(step, 0)
        advance_row(step, SIDE - 1)

    def interior(step):
        def body(i, carry):
            advance_row(step, i)
            return carry
        lax.fori_loop(1, SIDE - 1, body, 0, unroll=2)

    for step in range(STEPS - 1):
        advance_ends(step)
        start_halo(step + 1, (0, 1))
        column_out[step + 1, 0] = advance_column(step, 0)
        column_out[step + 1, 1] = advance_column(step, SIDE - 1)
        start_halo(step + 1, (2, 3))
        if step == 0:
            for i, ring in enumerate(rings):
                pl.semaphore_wait(known.at[0, i], 2)
                greet_ring(ring, known.at[1, i], 2)
        if step == 1:
            for i in range(len(rings)):
                pl.semaphore_wait(known.at[1, i], 2)
            greet_ring("z", known.at[2, 2], 2)
        interior(step)

    final = STEPS - 1
    interior(final)
    advance_ends(final)
    for cell in (0, SIDE - 1):
        states[STEPS][column(cell), :] = advance_column(final, cell) * last_scale

    slots = observed.shape[0]

    def pick(s, carry):
        cell = cells_ref[0, s]
        row = (cell // SIDE + 1) * PITCH + EDGE + lax.rem(cell, SIDE)
        observed[pl.ds(s, 1), :] = state3[pl.ds(row, 1), :]
        return carry

    for small in smalls[1:]:
        small.wait()
    lax.fori_loop(0, slots, pick, 0, unroll=16)

    seen = observed[...].T
    members_total = seen.shape[0]
    seen_mean = jnp.sum(seen, axis=0, keepdims=True) / members_total
    live = lax.broadcasted_iota(jnp.int32, (1, slots), 1) < count_ref[0, 0]
    weight = weight_ref[...]
    scaled = (seen - seen_mean) * jnp.where(live, weight / math.sqrt(total_slots), 0.0)
    innovation = jnp.where(live, weight * (value_ref[...] - seen_mean), 0.0)
    left = jnp.concatenate([scaled, jnp.broadcast_to(innovation, (8, slots))], axis=0)
    nt = (((1,), (1,)), ((), ()))
    gram = lax.dot_general(left, scaled, nt, precision=HIGHEST, preferred_element_type=jnp.float32)
    rows = members_total // n_gy
    for j in range(n_gy):
        parts[j, 0:rows, :] = gram[j * rows : (j + 1) * rows, :]
        parts[j, rows : rows + 1, :] = gram[members_total : members_total + 1, :]

    def exchange(count, me, peer, device, source, target, send, recv):
        def copy(i, slot):
            return pltpu.make_async_remote_copy(
                src_ref=source(peer(i)), dst_ref=target.at[slot],
                send_sem=send.at[peer(i)], recv_sem=recv.at[slot],
                device_id=device(peer(i)), device_id_type=MESH,
            )

        def begin():
            def body(i, carry):
                half = (i + 1) // 2
                copy(count // 2 + half * (1 - 2 * lax.rem(i, 2)), me).start()
                return carry
            lax.fori_loop(0, count - 1, body, 0)

        def end():
            def body(i, carry):
                copy(i, peer(i)).wait_recv()
                copy(i, me).wait_send()
                return carry
            lax.fori_loop(1, count, body, 0)

        return begin, end

    def total(ref, count):
        out = ref[0]
        for j in range(1, count):
            out = out + ref[j]
        return out

    gy_begin, gy_end = exchange(
        n_gy, gy, gy_peer, lambda p: (gx, p), lambda p: parts.at[p], from_gy, gy_send, gy_recv
    )
    y_begin, y_end = exchange(
        ny, y, y_peer, lambda p: (p * nz + z, gy), lambda p: held_y, from_y, y_send, y_recv
    )
    z_begin, z_end = exchange(
        nz, z, z_peer, lambda p: (y * nz + p, gy), lambda p: held_z, from_z, z_send, z_recv
    )
    back_begin, back_end = exchange(
        n_gy, gy, gy_peer, lambda p: (gx, p), lambda p: held_gy, whole, back_send, back_recv
    )

    def anomalies(i, carry):
        block = state3[pl.ds(pl.multiple_of((i + 1) * PITCH + EDGE, 8), SIDE), :]
        average = jnp.sum(block, axis=1, keepdims=True) / members_total
        hi, lo = split(block - average)
        at = pl.ds(pl.multiple_of(i * SIDE, SIDE), SIDE)
        anom[at, 0:128] = hi
        anom[at, 128:256] = lo
        mean_out[pl.ds(i, 1), :] = jnp.sum(jnp.where(eye, average, 0.0), axis=0, keepdims=True)
        return carry

    gy_begin()
    from_gy[gy] = parts[gy]
    lax.fori_loop(0, SIDE // 2, anomalies, 0, unroll=8)
    gy_end()
    held_y[...] = total(from_gy, n_gy)
    y_begin()
    from_y[y] = held_y[...]
    lax.fori_loop(SIDE // 2, SIDE, anomalies, 0, unroll=8)
    store = pltpu.make_async_copy(anom, anom_hbm, sem_anom)
    store.start()
    y_end()
    held_z[...] = total(from_y, ny)
    pl.semaphore_wait(known.at[2, 2], 2)
    z_begin()
    from_z[z] = held_z[...]
    z_end()
    held_gy[...] = total(from_z, nz)
    back_begin()
    whole[gy] = held_gy[...]
    back_end()
    gram_out[...] = whole[...]
    store.wait()
    for step in range(STEPS):
        await_sent(step)


def keep(array):
    return pltpu.with_memory_space_constraint(array, pltpu.HBM)


def forecast(nz, n_gx, n_gy, members, courant, cells, count, value, weight):
    ny = n_gx // nz
    piece = (128 // n_gy + 1, 128)
    f32 = jnp.float32
    state = pltpu.VMEM(((SIDE + 2) * PITCH, 128), f32)
    dma = pltpu.SemaphoreType.DMA
    vmem, smem, hbm, far = (
        pl.BlockSpec(memory_space=s) for s in (pltpu.VMEM, pltpu.SMEM, pl.ANY, pltpu.HBM)
    )
    return pl.pallas_call(
        functools.partial(forecast_kernel, nz, 128 * n_gx * n_gy),
        out_shape=(
            jax.ShapeDtypeStruct((n_gy,) + piece, f32),
            jax.ShapeDtypeStruct((SIDE * SIDE, 256), jnp.bfloat16),
            jax.ShapeDtypeStruct((SIDE, SIDE), f32),
        ),
        in_specs=[far, far, far, smem, far, far],
        out_specs=(vmem, hbm, vmem),
        scratch_shapes=[
            pltpu.VMEM((SIDE * SIDE, 128), jnp.bfloat16),
            pltpu.VMEM((2, SIDE, SIDE), f32),
            pltpu.SMEM((1, 128), jnp.int32),
            pltpu.VMEM((1, 128), f32),
            pltpu.VMEM((1, 128), f32),
            state, state, state, state,
            pltpu.VMEM((SIDE * SIDE, 128), f32),
            pltpu.VMEM((SIDE * SIDE, 128), f32),
            pltpu.VMEM((STEPS, 2, SIDE, 128), f32),
            pltpu.VMEM((STEPS, 2, SIDE, 128), f32),
            pltpu.VMEM((128, 128), f32),
            pltpu.VMEM((SIDE * SIDE, 256), jnp.bfloat16),
            pltpu.VMEM((n_gy,) + piece, f32),
            pltpu.VMEM((n_gy,) + piece, f32),
            pltpu.VMEM(piece, f32),
            pltpu.VMEM((ny,) + piece, f32),
            pltpu.VMEM(piece, f32),
            pltpu.VMEM((nz,) + piece, f32),
            pltpu.VMEM(piece, f32),
            pltpu.VMEM((n_gy,) + piece, f32),
            pltpu.SemaphoreType.REGULAR((3, 3)),
            dma, dma((4,)), dma,
            dma((STEPS, 4)), dma((STEPS, 4)),
            dma((n_gy,)), dma((n_gy,)),
            dma((ny,)), dma((ny,)),
            dma((nz,)), dma((nz,)),
            dma((n_gy,)), dma((n_gy,)),
        ],
        compiler_params=pltpu.CompilerParams(
            collective_id=0, has_side_effects=True, vmem_limit_bytes=40 * 2**20
        ),
    )(keep(members), keep(courant), keep(cells), count, keep(value), keep(weight))


def shards(nz, n_gx, n_gy, members, courant, obs_cells, obs_count, obs_value, obs_weight):
    tile_rows, tile_cols, member_total = members.shape
    flat = members.reshape(tile_rows * tile_cols, member_total)
    gram, anom, mean = forecast(
        nz, n_gx, n_gy, flat, courant,
        obs_cells.reshape(1, -1), obs_count, obs_value.reshape(1, -1), obs_weight.reshape(1, -1),
    )
    out_mean, out_anom = transform(gram, anom, mean)
    return out_mean, out_anom.reshape(members.shape)


Z_CHIPS = 12


def solution(mesh):
    n_gx, n_gy = mesh.shape["gx"], mesh.shape["gy"]
    in_specs = (
        P("gx", "gy", None),
        P(None, "gx", "gy"),
        P("gx", "gy", None),
        P("gx", "gy"),
        P("gx", "gy", None),
        P("gx", "gy", None),
    )
    out_specs = (P("gx", "gy"), P("gx", "gy", None))
    body = functools.partial(shards, Z_CHIPS, n_gx, n_gy)
    return jax.shard_map(body, mesh=mesh, in_specs=in_specs, out_specs=out_specs, check_vma=False)
```
